256 devices in a mesh: chan: 128 (over y_lo, x, z, core), tm: 2 (over y_hi).
Axes of the slice: x: 4, y: 4 (y_hi: 2, y_lo: 2; y = y_hi * 2 + y_lo), z: 8, core: 2. Of those that a mesh axis runs over, the one named last changes fastest.
Arguments:
- voltages: int32 [2, 512, 262144], P(None, 'chan', 'tm'), may hold values from -8 to 7
Outputs:
- visibilities: float32 [2, 1024, 512, 512], P(None, 'chan', 'tm')
The draws below stay inside these ranges and needn't reach their ends.
Inputs may be any that keep to these rules, and one draw needn't show every extreme that they name: `voltages`: 4-bit two's complement samples.
All inputs are finite; a program needn't handle non-finite values.
Results may differ from the reference program's by a relative error of at most 0.001.
Values may be sent and summed in bfloat16 or wider, within the bound.
No kernel may reach another device: no remote copies, remote signals or barrier semaphores. Data moves between devices by JAX's collectives and lax.ppermute only.
A program may use at most 128 MiB of HBM per device.

```python
import jax
import jax.numpy as jnp
from jax import lax

NCH = 1024
TAPS = 4
INPUTS = 512
NTOT = 256
SAMPLES = 262144


def place_ends(values, own_key, low, largest):
    longest = values.shape.index(max(values.shape))
    spots = []
    for shift in (0, 1):
        where = [jax.random.randint(jax.random.fold_in(own_key, axis), (), 0, length) for axis, length in enumerate(values.shape)]
        where[longest] = (where[longest] + shift) % values.shape[longest]
        spots.append(tuple(where))
    return values.at[spots[0]].set(low).at[spots[1]].set(largest)


def setup_inputs(seed: int = 0) -> dict:
    keys = jax.random.split(jax.random.key(seed), 2)
    voltages = place_ends(jax.random.randint(keys[0], (2, INPUTS, SAMPLES), -8, 8), jax.random.fold_in(keys[0], 1), -8, 7).astype(jnp.int32)
    return {"voltages": voltages}


def make_taps(nch):
    k = jnp.arange(TAPS * nch, dtype=jnp.float32)
    x = (k - 2.0 * nch + 0.5) / nch
    window = 0.54 - 0.46 * jnp.cos(2.0 * jnp.pi * (k + 0.5) / (TAPS * nch))
    return (jnp.sinc(x) * window).reshape(TAPS, nch)

def correlate_block(block):
    real_part = block[:, 0].astype(jnp.float32)
    imag_part = block[:, 1].astype(jnp.float32)
    vis_real = jnp.einsum('cas,cbs->cab', real_part, real_part) + jnp.einsum('cas,cbs->cab', imag_part, imag_part)
    vis_imag = jnp.einsum('cas,cbs->cab', imag_part, real_part) - jnp.einsum('cas,cbs->cab', real_part, imag_part)
    return jnp.stack([vis_real, vis_imag], axis=0)

def reference(voltages):
    samples = voltages.astype(jnp.float32) * 0.25
    frames = samples.reshape(2, INPUTS, NTOT, NCH)
    padded = jnp.concatenate([jnp.zeros((2, INPUTS, TAPS - 1, NCH), jnp.float32), frames], axis=2)
    taps = make_taps(NCH)
    filtered = taps[0] * padded[:, :, 0:NTOT, :]
    for step in range(1, TAPS):
        filtered = filtered + taps[step] * padded[:, :, step:step + NTOT, :]
    spectra = jnp.fft.fft(filtered[0] + 1j * filtered[1], axis=-1) / jnp.sqrt(jnp.float32(NCH))
    spec_real = jnp.real(spectra).astype(jnp.bfloat16)
    spec_imag = jnp.imag(spectra).astype(jnp.bfloat16)
    stacked = jnp.stack([spec_real, spec_imag], axis=0)
    by_channel = jnp.transpose(stacked, (3, 0, 1, 2)).reshape(NCH // 8, 8, 2, INPUTS, NTOT)
    result = lax.map(correlate_block, by_channel)
    result = jnp.transpose(result, (1, 0, 2, 3, 4)).reshape(2, NCH, INPUTS, INPUTS)
    return result * (1.0 / NTOT)
```

```python
import jax
import jax.numpy as jnp
import numpy as np
from jax import lax
from jax.experimental import pallas as pl
from jax.experimental.pallas import tpu as pltpu
from jax.sharding import Mesh
from jax.sharding import PartitionSpec as P

NCH = 1024
TAPS = 4
RADIX = 8
FINE = NCH // RADIX
LANES = 128
NA = 4
SPEC = 128
STEP = 32
HIST = TAPS - 1
ROWS = RADIX * NA
GROUP = 64
PLANE = ("x", "z", "core")
FIRST = (0, 1, 2, 3, 4)
SECOND = (5, 6, 7)


def taps_table():
    k = np.arange(TAPS * NCH, dtype=np.float64)
    x = (k - 2.0 * NCH + 0.5) / NCH
    window = 0.54 - 0.46 * np.cos(2.0 * np.pi * (k + 0.5) / (TAPS * NCH))
    taps = (np.sinc(x) * window * 0.25).reshape(TAPS, RADIX, 1, LANES)
    return np.broadcast_to(taps, (TAPS, RADIX, NA, LANES)).reshape(TAPS, ROWS, LANES).astype(np.float32)


def turn_table():
    j = np.arange(RADIX)[:, None, None]
    q = np.arange(FINE)[None, :, None]
    l = np.arange(FINE)[None, None, :]
    angle = 2.0 * np.pi * ((l * (RADIX * q + j)) % NCH) / NCH
    cosine = np.cos(angle) / np.sqrt(NCH)
    sine = np.sin(angle) / np.sqrt(NCH)
    real = np.concatenate([cosine, sine], axis=2)
    imag = np.concatenate([-sine, cosine], axis=2)
    full = np.concatenate([real, imag], axis=1)
    high = full.astype(jnp.bfloat16)
    low = (full - high.astype(np.float64)).astype(jnp.bfloat16)
    return np.stack([high, low], axis=1)


def gather_table():
    table = np.zeros((256, 256), np.float32)
    for p in range(2):
        for r in range(32):
            for a in range(NA):
                table[p * 128 + r * NA + a, r * 8 + p * NA + a] = 1.0
    return table.astype(jnp.bfloat16)


def butterfly(x):
    def add(u, v):
        return (u[0] + v[0], u[1] + v[1])

    def sub(u, v):
        return (u[0] - v[0], u[1] - v[1])

    def minus_i(u):
        return (u[1], -u[0])

    def four(a, b, c, d):
        s, t = add(a, c), sub(a, c)
        u, v = add(b, d), minus_i(sub(b, d))
        return add(s, u), add(t, v), sub(s, u), sub(t, v)

    half = np.float32(np.sqrt(0.5))
    even = four(x[0], x[2], x[4], x[6])
    odd = four(x[1], x[3], x[5], x[7])
    o1 = ((odd[1][0] + odd[1][1]) * half, (odd[1][1] - odd[1][0]) * half)
    o2 = minus_i(odd[2])
    o3 = ((odd[3][1] - odd[3][0]) * half, -(odd[3][0] + odd[3][1]) * half)
    odd = (odd[0], o1, o2, o3)
    return [add(even[i], odd[i]) for i in range(4)] + [sub(even[i], odd[i]) for i in range(4)]


def channel_kernel(place, order, volts, tail, taps, turn, *rest):
    outs, (ext, filt, high, low, spread) = rest[:-5], rest[-5:]
    step = pl.program_id(0)

    @pl.when(step == 0)
    def _():
        ext[:, : HIST * ROWS, :] = tail[...].astype(jnp.float32)

    @pl.when(step < SPEC // STEP)
    def _():
        for p in range(2):

            @pl.loop(0, STEP // 4)
            def _(i):
                base = pl.multiple_of(i * 4 * ROWS, 4 * ROWS)
                ext[p, pl.ds(HIST * ROWS + base, 4 * ROWS), :] = volts[
                    p, pl.ds(base, 4 * ROWS), :
                ].astype(jnp.float32)

            @pl.loop(0, STEP // 4)
            def _(i):
                base = pl.multiple_of(i * 4 * ROWS, 4 * ROWS)
                for piece in range(ROWS // 8):
                    weights = [taps[t, piece * 8 : piece * 8 + 8, :] for t in range(TAPS)]
                    frames = [
                        ext[p, pl.ds(base + (s * ROWS + piece * 8), 8), :] for s in range(4 + HIST)
                    ]
                    for s in range(4):
                        total = weights[0] * frames[s]
                        for t in range(1, TAPS):
                            total = total + weights[t] * frames[s + t]
                        filt[p, pl.ds(base + (s * ROWS + piece * 8), 8), :] = total

            ext[p, : HIST * ROWS, :] = ext[p, STEP * ROWS :, :]

        for a in range(NA):
            for part in range(STEP // 16):
                x = [
                    tuple(
                        filt[p, pl.ds(part * 16 * ROWS + m * NA + a, 16, stride=ROWS), :]
                        for p in range(2)
                    )
                    for m in range(RADIX)
                ]
                y = butterfly(x)
                row = pl.multiple_of(a * SPEC + step * STEP + part * 16, 16)
                for j in range(RADIX):
                    for p in range(2):
                        value = y[j][p]
                        top = value.astype(jnp.bfloat16)
                        rest_ = (value - top.astype(jnp.float32)).astype(jnp.bfloat16)
                        high[j, pl.ds(row, 16), p * LANES : (p + 1) * LANES] = top
                        low[j, pl.ds(row, 16), p * LANES : (p + 1) * LANES] = rest_

    @pl.when(step >= SPEC // STEP)
    def _():
        now = order[step - SPEC // STEP]
        mine = place[0]
        rows = []
        for kind in range(2):
            pieces = []
            for p in range(2):
                for slot in range(2):
                    half = mine if slot == 0 else 1 - mine
                    start = pl.multiple_of(p * FINE + half * GROUP, GROUP)
                    pieces.append(turn[0, kind, pl.ds(start, GROUP), :])
            rows.append(jnp.concatenate(pieces, axis=0))

        def dot(left, right):
            return lax.dot_general(
                left, right, (((1,), (1,)), ((), ())), preferred_element_type=jnp.float32
            )

        tops = high[now]
        spectra = dot(rows[0], tops) + (dot(rows[1], tops) + dot(rows[0], low[now]))
        for p in range(2):
            for slot in range(2):
                for a in range(NA):
                    spread[
                        pl.ds(slot * GROUP * 8 + p * NA + a, GROUP, stride=8), :
                    ] = spectra[
                        (p * 2 + slot) * GROUP : (p * 2 + slot + 1) * GROUP,
                        a * SPEC : (a + 1) * SPEC,
                    ]
        for slot in range(2):
            block = spread[slot * GROUP * 8 : (slot + 1) * GROUP * 8, :]
            block = block.reshape(GROUP, 8, LANES).astype(jnp.bfloat16)
            at = step - SPEC // STEP
            if len(outs) == 1:
                outs[0][:, slot, 0] = block
            else:
                cut = len(SECOND)

                @pl.when(at < len(FIRST))
                def _():
                    outs[0][:, slot, 0] = block

                @pl.when(at >= len(FIRST))
                def _():
                    outs[1][:, slot, 0] = block


def channelize(place, volts, tail):
    lead = SPEC // STEP
    order = np.array(FIRST + SECOND, np.int32)
    sizes = [len(FIRST), len(SECOND)] if SECOND else [len(FIRST)]
    starts = [0, len(FIRST)]

    def out_map(start, size):
        return lambda i, place, order: (0, 0, jnp.clip(i - lead - start, 0, size - 1), 0, 0)

    return pl.pallas_call(
        channel_kernel,
        grid_spec=pltpu.PrefetchScalarGridSpec(
            num_scalar_prefetch=2,
            grid=(lead + RADIX,),
            in_specs=[
                pl.BlockSpec((2, STEP * ROWS, LANES), lambda i, *_: (0, jnp.minimum(i, lead - 1), 0)),
                pl.BlockSpec((2, HIST * ROWS, LANES), lambda i, *_: (0, 0, 0)),
                pl.BlockSpec((TAPS, ROWS, LANES), lambda i, *_: (0, 0, 0)),
                pl.BlockSpec(
                    (1, 2, 2 * FINE, 2 * FINE),
                    lambda i, place, order: (order[jnp.maximum(i - lead, 0)], 0, 0, 0),
                ),
            ],
            out_specs=[
                pl.BlockSpec((GROUP, 2, 1, 8, LANES), out_map(start, size))
                for start, size in zip(starts, sizes)
            ],
            scratch_shapes=[
                pltpu.VMEM((2, (HIST + STEP) * ROWS, LANES), jnp.float32),
                pltpu.VMEM((2, STEP * ROWS, LANES), jnp.float32),
                pltpu.VMEM((RADIX, NA * SPEC, 2 * LANES), jnp.bfloat16),
                pltpu.VMEM((RADIX, NA * SPEC, 2 * LANES), jnp.bfloat16),
                pltpu.VMEM((2 * GROUP * 8, LANES), jnp.float32),
            ],
        ),
        out_shape=[
            jax.ShapeDtypeStruct((GROUP, 2, size, 8, LANES), jnp.bfloat16) for size in sizes
        ],
        compiler_params=pltpu.CompilerParams(
            dimension_semantics=("arbitrary",), vmem_limit_bytes=40 * 1024 * 1024
        ),
        cost_estimate=pl.CostEstimate(
            flops=2 * 10**9, bytes_accessed=8 * 1024 * 1024, transcendentals=0
        ),
        name="channelize",
    )(place, jnp.asarray(order), volts, tail, jnp.asarray(taps_table()), jnp.asarray(turn_table()))


def correlate_kernel(scale, place, same, far, near, cross, table, *rest):
    out, stage = rest[-2], rest[-1]
    mine, time = place[0], place[1]
    for kind, (here, there) in enumerate(((same, far), (near, cross))):
        group = mine if kind == 0 else 1 - mine
        left = here[...].reshape(GROUP * 8, LANES)
        right = there[...].reshape(GROUP * 8, LANES)
        for half in range(2):
            block = jnp.concatenate(
                [left[half * 256 : half * 256 + 256], right[half * 256 : half * 256 + 256]], axis=1
            )
            sorted_ = jnp.dot(table[...], block, preferred_element_type=jnp.float32)
            sorted_ = sorted_.astype(jnp.bfloat16)
            for p in range(2):
                stage[group, half * 128 : half * 128 + 128, p * 256 : p * 256 + 256] = sorted_[
                    p * 128 : p * 128 + 128
                ]

    rows = stage[time]
    turned = jnp.concatenate([rows[:, 256:], -rows[:, :256]], axis=1)

    def dot(left, right):
        return lax.dot_general(
            left, right, (((1,), (1,)), ((), ())), preferred_element_type=jnp.float32
        )

    for group in range(2):
        columns = stage[group]
        out[0, 0, :, group * 256 : group * 256 + 256] = dot(rows, columns) * scale
        out[1, 0, :, group * 256 : group * 256 + 256] = dot(turned, columns) * scale


def correlate(place, scale, first, count, own, far, near, cross, earlier):
    block = (GROUP, 1, 8, LANES)
    in_specs = [
        pl.BlockSpec((GROUP, 1, 1, 8, LANES), lambda i, *_: (0, 0, i, 0, 0)),
        pl.BlockSpec(block, lambda i, *_: (0, i, 0, 0)),
        pl.BlockSpec(block, lambda i, *_: (0, i, 0, 0)),
        pl.BlockSpec(block, lambda i, *_: (0, i, 0, 0)),
        pl.BlockSpec((256, 256), lambda i, *_: (0, 0)),
    ]
    operands = [place, own, far, near, cross, jnp.asarray(gather_table())]
    aliases = {}
    if earlier is not None:
        in_specs.append(pl.BlockSpec(memory_space=pl.ANY))
        aliases = {len(operands): 0}
        operands.append(earlier)

    def kernel(*refs):
        correlate_kernel(scale, *refs)

    return pl.pallas_call(
        kernel,
        grid_spec=pltpu.PrefetchScalarGridSpec(
            num_scalar_prefetch=1,
            grid=(count,),
            in_specs=in_specs,
            out_specs=pl.BlockSpec((2, 1, 256, 512), lambda i, *_: (0, first + i, 0, 0)),
            scratch_shapes=[pltpu.VMEM((2, 256, 512), jnp.bfloat16)],
        ),
        out_shape=jax.ShapeDtypeStruct((2, 8, 256, 512), jnp.float32),
        input_output_aliases=aliases,
        compiler_params=pltpu.CompilerParams(
            dimension_semantics=("arbitrary",), vmem_limit_bytes=24 * 1024 * 1024
        ),
        cost_estimate=pl.CostEstimate(
            flops=count * 4 * 10**8, bytes_accessed=count * 3 * 512 * 1024, transcendentals=0
        ),
        name="correlate",
    )(*operands)


def exchange(near_part, far_part):
    flip = [(0, 1), (1, 0)]
    both = [(0, 3), (3, 0), (1, 2), (2, 1)]
    near = lax.ppermute(near_part, "y_lo", flip)
    cross = lax.ppermute(near_part, ("y_lo", "tm"), both)
    far = lax.ppermute(far_part, "tm", flip)
    return far, near, cross


def local(voltages):
    tiles = voltages.shape[2] // LANES
    volts = voltages.reshape(2, NA, tiles, LANES).transpose(0, 2, 1, 3).reshape(2, tiles * NA, LANES)
    tail = lax.ppermute(volts[:, (SPEC - HIST) * ROWS :], "tm", [(0, 1)])
    place = jnp.stack([lax.axis_index("y_lo"), lax.axis_index("tm")]).astype(jnp.int32)
    scale = np.float32(1.0 / (SPEC * lax.axis_size("tm")))
    parts = channelize(place, volts, tail)
    result = None
    first = 0
    for part in parts:
        turned = lax.all_to_all(part, PLANE, split_axis=0, concat_axis=0, tiled=True)
        far, near, cross = exchange(turned[:, 1], turned[:, 0])
        count = part.shape[2]
        result = correlate(place, scale, first, count, turned, far, near, cross, result)
        first += count
    return result


def solution(mesh):
    names = ("y_lo", "x", "z", "core", "tm")
    fine = Mesh(mesh.devices.reshape(2, 4, 8, 2, 2), names)
    chan = names[:-1]
    return jax.shard_map(
        local,
        mesh=fine,
        in_specs=P(None, chan, "tm"),
        out_specs=P(None, chan, "tm", None),
        check_vma=False,
    )
```

```python
import jax
import jax.numpy as jnp
import numpy as np
from jax import lax
from jax.experimental import pallas as pl
from jax.experimental.pallas import tpu as pltpu
from jax.sharding import Mesh
from jax.sharding import PartitionSpec as P

NCH = 1024
TAPS = 4
RADIX = 8
FINE = NCH // RADIX
LANES = 128
NA = 4
SPEC = 128
STEP = 32
BATCH = 8
HIST = TAPS - 1
ROWS = RADIX * NA
GROUP = 64
PLANE = ("x", "z", "core")
PLANE_FIRST = (0, 1, 2, 3, 4)
Y_FIRST = (5, 6, 7)


def taps_table():
    k = jnp.arange(TAPS * NCH, dtype=jnp.float32)
    x = (k - 2.0 * NCH + 0.5) / NCH
    window = 0.54 - 0.46 * jnp.cos(2.0 * jnp.pi * (k + 0.5) / (TAPS * NCH))
    taps = (jnp.sinc(x) * window * 0.25).reshape(TAPS, RADIX, 1, LANES)
    return jnp.broadcast_to(taps, (TAPS, RADIX, NA, LANES)).reshape(TAPS, ROWS, LANES)


def turn_table():
    j = np.arange(RADIX)[:, None, None]
    q = np.arange(FINE)[None, :, None]
    l = np.arange(FINE)[None, None, :]
    angle = 2.0 * np.pi * ((l * (RADIX * q + j)) % NCH) / NCH
    cosine = np.cos(angle) / np.sqrt(NCH)
    sine = np.sin(angle) / np.sqrt(NCH)
    real = np.concatenate([cosine, sine], axis=2)
    imag = np.concatenate([-sine, cosine], axis=2)
    full = np.concatenate([real, imag], axis=1)
    high = full.astype(jnp.bfloat16)
    low = (full - high.astype(np.float64)).astype(jnp.bfloat16)
    return np.stack([high, low], axis=1)


def gather_table():
    table = np.zeros((256, 256), np.float32)
    for p in range(2):
        for r in range(32):
            for a in range(NA):
                table[p * 128 + r * NA + a, r * 8 + p * NA + a] = 1.0
    return table.astype(jnp.bfloat16)


def butterfly(x):
    def add(u, v):
        return (u[0] + v[0], u[1] + v[1])

    def sub(u, v):
        return (u[0] - v[0], u[1] - v[1])

    def minus_i(u):
        return (u[1], -u[0])

    def four(a, b, c, d):
        s, t = add(a, c), sub(a, c)
        u, v = add(b, d), minus_i(sub(b, d))
        return add(s, u), add(t, v), sub(s, u), sub(t, v)

    half = np.float32(np.sqrt(0.5))
    even = four(x[0], x[2], x[4], x[6])
    odd = four(x[1], x[3], x[5], x[7])
    o1 = ((odd[1][0] + odd[1][1]) * half, (odd[1][1] - odd[1][0]) * half)
    o2 = minus_i(odd[2])
    o3 = ((odd[3][1] - odd[3][0]) * half, -(odd[3][0] + odd[3][1]) * half)
    odd = (odd[0], o1, o2, o3)
    return [add(even[i], odd[i]) for i in range(4)] + [sub(even[i], odd[i]) for i in range(4)]


def channel_kernel(place, volts, tail, taps, turn, stay, leave, rest, raw, filt, high, low, table, spread, arrived):
    def chunk_copy(c):
        at = pl.multiple_of(c * STEP * ROWS, STEP * ROWS)
        return pltpu.make_async_copy(
            volts.at[:, pl.ds(at, STEP * ROWS), :],
            raw.at[:, pl.ds(HIST * ROWS + at, STEP * ROWS), :],
            arrived.at[c],
        )

    table_copy = pltpu.make_async_copy(turn, table, arrived.at[SPEC // STEP])
    for c in range(SPEC // STEP):
        chunk_copy(c).start()
    table_copy.start()
    raw[:, : HIST * ROWS, :] = tail[...]

    @pl.loop(0, SPEC // STEP)
    def _(c):
        chunk_copy(c).wait()
        for p in range(2):

            @pl.loop(0, STEP // BATCH)
            def _(i):
                into = pl.multiple_of(i * BATCH * ROWS, BATCH * ROWS)
                base = pl.multiple_of(c * STEP * ROWS + into, BATCH * ROWS)
                for piece in range(ROWS // 8):
                    weights = [taps[t, piece * 8 : piece * 8 + 8, :] for t in range(TAPS)]
                    frames = [
                        raw[p, pl.ds(base + (s * ROWS + piece * 8), 8), :].astype(jnp.float32)
                        for s in range(BATCH + HIST)
                    ]
                    for s in range(BATCH):
                        total = weights[0] * frames[s]
                        for t in range(1, TAPS):
                            total = total + weights[t] * frames[s + t]
                        filt[p, pl.ds(into + (s * ROWS + piece * 8), 8), :] = total

        for a in range(NA):
            for part in range(STEP // 16):
                x = [
                    tuple(
                        filt[p, pl.ds(part * 16 * ROWS + m * NA + a, 16, stride=ROWS), :]
                        for p in range(2)
                    )
                    for m in range(RADIX)
                ]
                y = butterfly(x)
                row = pl.multiple_of(a * SPEC + c * STEP + part * 16, 16)
                for j in range(RADIX):
                    for p in range(2):
                        value = y[j][p]
                        top = value.astype(jnp.bfloat16)
                        left_over = (value - top.astype(jnp.float32)).astype(jnp.bfloat16)
                        high[j, pl.ds(row, 16), p * LANES : (p + 1) * LANES] = top
                        low[j, pl.ds(row, 16), p * LANES : (p + 1) * LANES] = left_over

    table_copy.wait()
    mine = place[0]

    def dot(left, right):
        return lax.dot_general(
            left, right, (((1,), (1,)), ((), ())), preferred_element_type=jnp.float32
        )

    def transform(j):
        rows = []
        for kind in range(2):
            pieces = []
            for p in range(2):
                for slot in range(2):
                    half = mine if slot == 0 else 1 - mine
                    start = pl.multiple_of(p * FINE + half * GROUP, GROUP)
                    pieces.append(table[j, kind, pl.ds(start, GROUP), :])
            rows.append(jnp.concatenate(pieces, axis=0))
        tops = high[j]
        spectra = dot(rows[0], tops) + (dot(rows[1], tops) + dot(rows[0], low[j]))
        blocks = []
        for slot in range(2):
            for p in range(2):
                for a in range(NA):
                    spread[
                        pl.ds(slot * GROUP * 8 + p * NA + a, GROUP, stride=8), :
                    ] = spectra[
                        (p * 2 + slot) * GROUP : (p * 2 + slot + 1) * GROUP,
                        a * SPEC : (a + 1) * SPEC,
                    ]
            block = spread[slot * GROUP * 8 : (slot + 1) * GROUP * 8, :]
            blocks.append(block.reshape(GROUP, 8, LANES).astype(jnp.bfloat16))
        return blocks

    for i, j in enumerate(PLANE_FIRST):
        blocks = transform(j)
        for slot in range(2):
            rest[:, slot, i] = blocks[slot]

    for i, j in enumerate(Y_FIRST):
        stay[:, i], leave[:, i] = transform(j)


def channelize(place, volts, tail):
    few, many = len(Y_FIRST), len(PLANE_FIRST)
    vmem = pl.BlockSpec(memory_space=pltpu.VMEM)
    hbm = pl.BlockSpec(memory_space=pltpu.HBM)
    return pl.pallas_call(
        channel_kernel,
        in_specs=[pl.BlockSpec(memory_space=pltpu.SMEM), hbm, vmem, vmem, hbm],
        out_specs=[vmem, vmem, vmem],
        scratch_shapes=[
            pltpu.VMEM((2, (HIST + SPEC) * ROWS, LANES), jnp.int32),
            pltpu.VMEM((2, STEP * ROWS, LANES), jnp.float32),
            pltpu.VMEM((RADIX, NA * SPEC, 2 * LANES), jnp.bfloat16),
            pltpu.VMEM((RADIX, NA * SPEC, 2 * LANES), jnp.bfloat16),
            pltpu.VMEM((RADIX, 2, 2 * FINE, 2 * FINE), jnp.bfloat16),
            pltpu.VMEM((2 * GROUP * 8, LANES), jnp.float32),
            pltpu.SemaphoreType.DMA((SPEC // STEP + 1,)),
        ],
        out_shape=[
            jax.ShapeDtypeStruct((GROUP, few, 8, LANES), jnp.bfloat16),
            jax.ShapeDtypeStruct((GROUP, few, 8, LANES), jnp.bfloat16),
            jax.ShapeDtypeStruct((GROUP, 2, many, 8, LANES), jnp.bfloat16),
        ],
        compiler_params=pltpu.CompilerParams(vmem_limit_bytes=52 * 1024 * 1024),
        cost_estimate=pl.CostEstimate(
            flops=2 * 10**9, bytes_accessed=8 * 1024 * 1024, transcendentals=0
        ),
        name="channelize",
    )(place, volts, tail, taps_table(), jnp.asarray(turn_table()))


def correlate_kernel(scale, first, count, picks, place, *refs):
    operands, table, out = refs[: len(picks)], refs[len(picks)], refs[-3]
    held, sent = refs[-2:]
    mine, time = place[0], place[1]
    low_first = mine == 0

    def dot(left, right):
        return lax.dot_general(
            left, right, (((1,), (1,)), ((), ())), preferred_element_type=jnp.float32
        )

    def give(i):
        slot = i % 2
        return pltpu.make_async_copy(held.at[slot], out.at[:, first + i], sent.at[slot])

    for i in range(count):
        sets = []
        for kind in range(2):
            pair = [
                ref[:, at, i] if at is not None else ref[:, i]
                for ref, at in zip(operands[2 * kind : 2 * kind + 2], picks[2 * kind : 2 * kind + 2])
            ]
            pair = [block.reshape(GROUP * 8, LANES) for block in pair]
            parts = ([], [])
            for half in range(2):
                block = jnp.concatenate([b[half * 256 : half * 256 + 256] for b in pair], axis=1)
                ordered = jnp.dot(table[...], block, preferred_element_type=jnp.float32)
                ordered = ordered.astype(jnp.bfloat16)
                for p in range(2):
                    parts[p].append(ordered[p * 128 : p * 128 + 128])
            sets.append(jnp.concatenate([jnp.concatenate(part, axis=0) for part in parts], axis=1))
        columns = [jnp.where(low_first, sets[0], sets[1]), jnp.where(low_first, sets[1], sets[0])]
        rows = jnp.where(time == 0, columns[0], columns[1])
        turned = jnp.concatenate([rows[:, 256:], -rows[:, :256]], axis=1)

        if i >= 2:
            give(i - 2).wait()
        slot = i % 2
        for group in range(2):
            at = slice(group * 256, group * 256 + 256)
            held[slot, 0, :, at] = dot(rows, columns[group]) * scale
            held[slot, 1, :, at] = dot(turned, columns[group]) * scale
        give(i).start()

    for i in range(max(count - 2, 0), count):
        give(i).wait()


def correlate(place, scale, first, count, kinds, earlier):
    vmem = pl.BlockSpec(memory_space=pltpu.VMEM)
    hbm = pl.BlockSpec(memory_space=pltpu.HBM)
    picks = [at for _, at in kinds]
    operands = [place, *(block for block, _ in kinds), jnp.asarray(gather_table())]
    in_specs = [pl.BlockSpec(memory_space=pltpu.SMEM)] + [vmem] * (len(operands) - 1)
    aliases = {}
    if earlier is not None:
        in_specs.append(hbm)
        aliases = {len(operands): 0}
        operands.append(earlier)

    def kernel(*refs):
        correlate_kernel(scale, first, count, picks, *refs)

    return pl.pallas_call(
        kernel,
        in_specs=in_specs,
        out_specs=hbm,
        scratch_shapes=[
            pltpu.VMEM((2, 2, 256, 512), jnp.float32),
            pltpu.SemaphoreType.DMA((2,)),
        ],
        out_shape=jax.ShapeDtypeStruct((2, 8, 256, 512), jnp.float32),
        input_output_aliases=aliases,
        compiler_params=pltpu.CompilerParams(vmem_limit_bytes=24 * 1024 * 1024),
        cost_estimate=pl.CostEstimate(
            flops=count * 4 * 10**8, bytes_accessed=count * 3 * 512 * 1024, transcendentals=0
        ),
        name="correlate",
    )(*operands)


def exchange(near_part, far_part):
    flip = [(0, 1), (1, 0)]
    both = [(0, 3), (3, 0), (1, 2), (2, 1)]
    near = lax.ppermute(near_part, "y_lo", flip)
    cross = lax.ppermute(near_part, ("y_lo", "tm"), both)
    far = lax.ppermute(far_part, "tm", flip)
    return far, near, cross


def local(voltages):
    tiles = voltages.shape[2] // LANES
    volts = voltages.reshape(2, NA, tiles, LANES).transpose(0, 2, 1, 3).reshape(2, tiles * NA, LANES)
    tail = lax.ppermute(volts[:, (SPEC - HIST) * ROWS :], "tm", [(0, 1)])
    place = jnp.stack([lax.axis_index("y_lo"), lax.axis_index("tm")]).astype(jnp.int32)
    scale = np.float32(1.0 / (SPEC * lax.axis_size("tm")))
    stay, leave, rest = channelize(place, volts, tail)
    over = lax.all_to_all(rest, PLANE, split_axis=0, concat_axis=0, tiled=True)
    early = jnp.stack([stay, *exchange(leave, stay)], axis=1)
    far, near, cross = exchange(over[:, 1], over[:, 0])
    early = lax.all_to_all(early, PLANE, split_axis=0, concat_axis=0, tiled=True)
    result = correlate(
        place, scale, 0, len(PLANE_FIRST), [(over, 0), (far, None), (near, None), (cross, None)], None
    )
    return correlate(
        place, scale, len(PLANE_FIRST), len(Y_FIRST), [(early, kind) for kind in range(4)], result
    )


def solution(mesh):
    names = ("y_lo", "x", "z", "core", "tm")
    fine = Mesh(mesh.devices.reshape(2, 4, 8, 2, 2), names)
    chan = names[:-1]
    return jax.shard_map(
        local,
        mesh=fine,
        in_specs=P(None, chan, "tm"),
        out_specs=P(None, chan, "tm", None),
        check_vma=False,
    )
```

```python
import jax
import jax.numpy as jnp
import numpy as np
from jax import lax
from jax.experimental import pallas as pl
from jax.experimental.pallas import tpu as pltpu
from jax.sharding import Mesh
from jax.sharding import PartitionSpec as P

NCH = 1024
TAPS = 4
RADIX = 8
FINE = NCH // RADIX
LANES = 128
NA = 4
SPEC = 128
STEP = 32
BATCH = 8
SLOTS = 5
VMEM_KIB = 50 * 1024
HIST = TAPS - 1
ROWS = RADIX * NA
GROUP = 64
PLANE = ("x", "z", "core")
PLANE_FIRST = (0, 1, 2, 3, 4)
Y_FIRST = (5, 6, 7)


def taps_table():
    k = jnp.arange(TAPS * NCH, dtype=jnp.float32)
    x = (k - 2.0 * NCH + 0.5) / NCH
    window = 0.54 - 0.46 * jnp.cos(2.0 * jnp.pi * (k + 0.5) / (TAPS * NCH))
    taps = (jnp.sinc(x) * window * 0.25).reshape(TAPS, RADIX, 1, LANES)
    return jnp.broadcast_to(taps, (TAPS, RADIX, NA, LANES)).reshape(TAPS, ROWS, LANES)


def turn_table():
    j = np.arange(RADIX)[:, None, None]
    q = np.arange(FINE)[None, :, None]
    l = np.arange(FINE)[None, None, :]
    angle = 2.0 * np.pi * ((l * (RADIX * q + j)) % NCH) / NCH
    cosine = np.cos(angle) / np.sqrt(NCH)
    sine = np.sin(angle) / np.sqrt(NCH)
    real = np.concatenate([cosine, sine], axis=2)
    imag = np.concatenate([-sine, cosine], axis=2)
    full = np.concatenate([real, imag], axis=1)
    high = full.astype(jnp.bfloat16)
    low = (full - high.astype(np.float64)).astype(jnp.bfloat16)
    blank = np.zeros_like(high)
    return np.stack([high, low, blank, blank], axis=1)


def gather_table():
    table = np.zeros((256, 256), np.float32)
    for p in range(2):
        for r in range(32):
            for a in range(NA):
                table[p * 128 + r * NA + a, r * 8 + p * NA + a] = 1.0
    return table.astype(jnp.bfloat16)


def butterfly(x):
    def add(u, v):
        return (u[0] + v[0], u[1] + v[1])

    def sub(u, v):
        return (u[0] - v[0], u[1] - v[1])

    def minus_i(u):
        return (u[1], -u[0])

    def four(a, b, c, d):
        s, t = add(a, c), sub(a, c)
        u, v = add(b, d), minus_i(sub(b, d))
        return add(s, u), add(t, v), sub(s, u), sub(t, v)

    half = np.float32(np.sqrt(0.5))
    even = four(x[0], x[2], x[4], x[6])
    odd = four(x[1], x[3], x[5], x[7])
    o1 = ((odd[1][0] + odd[1][1]) * half, (odd[1][1] - odd[1][0]) * half)
    o2 = minus_i(odd[2])
    o3 = ((odd[3][1] - odd[3][0]) * half, -(odd[3][0] + odd[3][1]) * half)
    odd = (odd[0], o1, o2, o3)
    return [add(even[i], odd[i]) for i in range(4)] + [sub(even[i], odd[i]) for i in range(4)]


def transform(mine, j, table, high, low, spread):
    def dot(left, right):
        return lax.dot_general(
            left, right, (((1,), (1,)), ((), ())), preferred_element_type=jnp.float32
        )

    rows = []
    for kind in range(2):
        pieces = []
        for p in range(2):
            for slot in range(2):
                half = mine if slot == 0 else 1 - mine
                start = pl.multiple_of(p * FINE + half * GROUP, GROUP)
                pieces.append(table[j, kind, pl.ds(start, GROUP), :])
        rows.append(jnp.concatenate(pieces, axis=0))
    tops = high[j]
    spectra = dot(rows[0], tops) + (dot(rows[1], tops) + dot(rows[0], low[j]))
    blocks = []
    for slot in range(2):
        for p in range(2):
            for a in range(NA):
                spread[
                    pl.ds(slot * GROUP * 8 + p * NA + a, GROUP, stride=8), :
                ] = spectra[
                    (p * 2 + slot) * GROUP : (p * 2 + slot + 1) * GROUP,
                    a * SPEC : (a + 1) * SPEC,
                ]
        block = spread[slot * GROUP * 8 : (slot + 1) * GROUP * 8, :]
        blocks.append(block.reshape(GROUP, 8, LANES).astype(jnp.bfloat16))
    return blocks


def channel_kernel(
    place, volts, tail, taps, turn, rest, late_high, late_low, raw, filt, high, low, table, spread, arrived
):
    def chunk_copy(c):
        at = pl.multiple_of(c * STEP * ROWS, STEP * ROWS)
        return pltpu.make_async_copy(
            volts.at[:, pl.ds(at, STEP * ROWS), :],
            raw.at[:, pl.ds(HIST * ROWS + at, STEP * ROWS), :],
            arrived.at[c],
        )

    table_copy = pltpu.make_async_copy(
        turn.at[pl.ds(0, len(PLANE_FIRST)), pl.ds(0, 2)], table, arrived.at[SPEC // STEP]
    )
    for c in range(SPEC // STEP):
        chunk_copy(c).start()
    table_copy.start()
    raw[:, : HIST * ROWS, :] = tail[...]

    @pl.loop(0, SPEC // STEP)
    def _(c):
        chunk_copy(c).wait()
        for p in range(2):

            @pl.loop(0, STEP // BATCH)
            def _(i):
                into = pl.multiple_of(i * BATCH * ROWS, BATCH * ROWS)
                base = pl.multiple_of(c * STEP * ROWS + into, BATCH * ROWS)
                for piece in range(ROWS // 8):
                    weights = [taps[t, piece * 8 : piece * 8 + 8, :] for t in range(TAPS)]
                    frames = [
                        raw[p, pl.ds(base + (s * ROWS + piece * 8), 8), :].astype(jnp.float32)
                        for s in range(BATCH + HIST)
                    ]
                    for s in range(BATCH):
                        total = weights[0] * frames[s]
                        for t in range(1, TAPS):
                            total = total + weights[t] * frames[s + t]
                        filt[p, pl.ds(into + (s * ROWS + piece * 8), 8), :] = total

        for a in range(NA):
            for part in range(STEP // 16):
                x = [
                    tuple(
                        filt[p, pl.ds(part * 16 * ROWS + m * NA + a, 16, stride=ROWS), :]
                        for p in range(2)
                    )
                    for m in range(RADIX)
                ]
                y = butterfly(x)
                row = pl.multiple_of(a * SPEC + c * STEP + part * 16, 16)
                for j in range(RADIX):
                    for p in range(2):
                        value = y[j][p]
                        top = value.astype(jnp.bfloat16)
                        left_over = (value - top.astype(jnp.float32)).astype(jnp.bfloat16)
                        at = (slice(p * LANES, (p + 1) * LANES),)
                        early = j < len(PLANE_FIRST)
                        here = j if early else j - len(PLANE_FIRST)
                        (high if early else late_high)[here, pl.ds(row, 16), *at] = top
                        (low if early else late_low)[here, pl.ds(row, 16), *at] = left_over

    table_copy.wait()
    for i in range(len(PLANE_FIRST)):
        blocks = transform(place[0], i, table, high, low, spread)
        for slot in range(2):
            rest[:, slot, i] = blocks[slot]


def late_kernel(place, turn, high, low, stay, leave, table, spread, arrived):
    table_copy = pltpu.make_async_copy(
        turn.at[pl.ds(len(PLANE_FIRST), len(Y_FIRST)), pl.ds(0, 2)], table, arrived
    )
    table_copy.start()
    table_copy.wait()
    for i in range(len(Y_FIRST)):
        stay[:, i], leave[:, i] = transform(place[0], i, table, high, low, spread)


def channelize(place, volts, tail, turn):
    few, many = len(Y_FIRST), len(PLANE_FIRST)
    vmem = pl.BlockSpec(memory_space=pltpu.VMEM)
    hbm = pl.BlockSpec(memory_space=pltpu.HBM)
    mixed = jax.ShapeDtypeStruct((few, NA * SPEC, 2 * LANES), jnp.bfloat16)
    return pl.pallas_call(
        channel_kernel,
        in_specs=[pl.BlockSpec(memory_space=pltpu.SMEM), hbm, vmem, vmem, hbm],
        out_specs=[vmem, vmem, vmem],
        scratch_shapes=[
            pltpu.VMEM((2, (HIST + SPEC) * ROWS, LANES), jnp.int32),
            pltpu.VMEM((2, STEP * ROWS, LANES), jnp.float32),
            pltpu.VMEM((many, NA * SPEC, 2 * LANES), jnp.bfloat16),
            pltpu.VMEM((many, NA * SPEC, 2 * LANES), jnp.bfloat16),
            pltpu.VMEM((many, 2, 2 * FINE, 2 * FINE), jnp.bfloat16),
            pltpu.VMEM((2 * GROUP * 8, LANES), jnp.float32),
            pltpu.SemaphoreType.DMA((SPEC // STEP + 1,)),
        ],
        out_shape=[jax.ShapeDtypeStruct((GROUP, 2, many, 8, LANES), jnp.bfloat16), mixed, mixed],
        compiler_params=pltpu.CompilerParams(vmem_limit_bytes=VMEM_KIB * 1024),
        cost_estimate=pl.CostEstimate(
            flops=2 * 10**9, bytes_accessed=8 * 1024 * 1024, transcendentals=0
        ),
        name="channelize",
    )(place, volts, tail, taps_table(), turn)


def channelize_late(place, turn, high, low):
    few = len(Y_FIRST)
    vmem = pl.BlockSpec(memory_space=pltpu.VMEM)
    hbm = pl.BlockSpec(memory_space=pltpu.HBM)
    block = jax.ShapeDtypeStruct((GROUP, few, 8, LANES), jnp.bfloat16)
    return pl.pallas_call(
        late_kernel,
        in_specs=[pl.BlockSpec(memory_space=pltpu.SMEM), hbm, vmem, vmem],
        out_specs=[vmem, vmem],
        scratch_shapes=[
            pltpu.VMEM((few, 2, 2 * FINE, 2 * FINE), jnp.bfloat16),
            pltpu.VMEM((2 * GROUP * 8, LANES), jnp.float32),
            pltpu.SemaphoreType.DMA(()),
        ],
        out_shape=[block, block],
        compiler_params=pltpu.CompilerParams(vmem_limit_bytes=24 * 1024 * 1024),
        cost_estimate=pl.CostEstimate(
            flops=6 * 10**8, bytes_accessed=3 * 1024 * 1024, transcendentals=0
        ),
        name="channelize_late",
    )(place, turn, high, low)


def correlate_kernel(scale, first, count, picks, place, *refs):
    operands, table, out = refs[: len(picks)], refs[len(picks)], refs[-3]
    held, sent = refs[-2:]
    mine, time = place[0], place[1]
    low_first = mine == 0

    def dot(left, right):
        return lax.dot_general(
            left, right, (((1,), (1,)), ((), ())), preferred_element_type=jnp.float32
        )

    def give(i, part):
        slot = i % SLOTS
        return pltpu.make_async_copy(
            held.at[slot, part], out.at[part, first + i], sent.at[slot, part]
        )

    for i in range(count):
        sets = []
        for kind in range(2):
            pair = [
                ref[:, at, i] if at is not None else ref[:, i]
                for ref, at in zip(operands[2 * kind : 2 * kind + 2], picks[2 * kind : 2 * kind + 2])
            ]
            pair = [block.reshape(GROUP * 8, LANES) for block in pair]
            parts = ([], [])
            for half in range(2):
                block = jnp.concatenate([b[half * 256 : half * 256 + 256] for b in pair], axis=1)
                ordered = jnp.dot(table[...], block, preferred_element_type=jnp.float32)
                ordered = ordered.astype(jnp.bfloat16)
                for p in range(2):
                    parts[p].append(ordered[p * 128 : p * 128 + 128])
            sets.append(jnp.concatenate([jnp.concatenate(part, axis=0) for part in parts], axis=1))
        columns = [jnp.where(low_first, sets[0], sets[1]), jnp.where(low_first, sets[1], sets[0])]
        rows = jnp.where(time == 0, columns[0], columns[1])
        turned = jnp.concatenate([rows[:, 256:], -rows[:, :256]], axis=1)

        slot = i % SLOTS
        for part, left in enumerate((rows, turned)):
            if i >= SLOTS:
                give(i - SLOTS, part).wait()
            for group in range(2):
                at = slice(group * 256, group * 256 + 256)
                held[slot, part, :, at] = dot(left, columns[group]) * scale
            give(i, part).start()
    for i in range(max(count - SLOTS, 0), count):
        for part in range(2):
            give(i, part).wait()


def correlate(place, scale, first, count, kinds, earlier):
    vmem = pl.BlockSpec(memory_space=pltpu.VMEM)
    hbm = pl.BlockSpec(memory_space=pltpu.HBM)
    picks = [at for _, at in kinds]
    operands = [place, *(block for block, _ in kinds), jnp.asarray(gather_table())]
    in_specs = [pl.BlockSpec(memory_space=pltpu.SMEM)] + [vmem] * (len(operands) - 1)
    aliases = {}
    if earlier is not None:
        in_specs.append(hbm)
        aliases = {len(operands): 0}
        operands.append(earlier)

    def kernel(*refs):
        correlate_kernel(scale, first, count, picks, *refs)

    return pl.pallas_call(
        kernel,
        in_specs=in_specs,
        out_specs=hbm,
        scratch_shapes=[
            pltpu.VMEM((SLOTS, 2, 256, 512), jnp.float32),
            pltpu.SemaphoreType.DMA((SLOTS, 2)),
        ],
        out_shape=jax.ShapeDtypeStruct((2, 8, 256, 512), jnp.float32),
        input_output_aliases=aliases,
        compiler_params=pltpu.CompilerParams(vmem_limit_bytes=24 * 1024 * 1024),
        cost_estimate=pl.CostEstimate(
            flops=count * 4 * 10**8, bytes_accessed=count * 3 * 512 * 1024, transcendentals=0
        ),
        name="correlate",
    )(*operands)


def exchange(near_part, far_part):
    flip = [(0, 1), (1, 0)]
    both = [(0, 3), (3, 0), (1, 2), (2, 1)]
    near = lax.ppermute(near_part, "y_lo", flip)
    cross = lax.ppermute(near_part, ("y_lo", "tm"), both)
    far = lax.ppermute(far_part, "tm", flip)
    return far, near, cross


def local(voltages):
    tiles = voltages.shape[2] // LANES
    volts = voltages.reshape(2, NA, tiles, LANES).transpose(0, 2, 1, 3).reshape(2, tiles * NA, LANES)
    tail = lax.ppermute(volts[:, (SPEC - HIST) * ROWS :], "tm", [(0, 1)])
    place = jnp.stack([lax.axis_index("y_lo"), lax.axis_index("tm")]).astype(jnp.int32)
    scale = np.float32(1.0 / (SPEC * lax.axis_size("tm")))
    turn = jnp.asarray(turn_table())
    rest, high, low = channelize(place, volts, tail, turn)
    stay, leave = channelize_late(place, turn, high, low)
    over = lax.all_to_all(rest, PLANE, split_axis=0, concat_axis=0, tiled=True)
    early = jnp.stack([stay, *exchange(leave, stay)], axis=1)
    far, near, cross = exchange(over[:, 1], over[:, 0])
    early = lax.all_to_all(early, PLANE, split_axis=0, concat_axis=0, tiled=True)
    result = correlate(
        place, scale, 0, len(PLANE_FIRST), [(over, 0), (far, None), (near, None), (cross, None)], None
    )
    return correlate(
        place, scale, len(PLANE_FIRST), len(Y_FIRST), [(early, kind) for kind in range(4)], result
    )


def solution(mesh):
    names = ("y_lo", "x", "z", "core", "tm")
    fine = Mesh(mesh.devices.reshape(2, 4, 8, 2, 2), names)
    chan = names[:-1]
    return jax.shard_map(
        local,
        mesh=fine,
        in_specs=P(None, chan, "tm"),
        out_specs=P(None, chan, "tm", None),
        check_vma=False,
    )
```

```python
import jax
import jax.numpy as jnp
import numpy as np
from jax import lax
from jax.experimental import pallas as pl
from jax.experimental.pallas import tpu as pltpu
from jax.sharding import Mesh
from jax.sharding import PartitionSpec as P

NCH = 1024
TAPS = 4
RADIX = 8
FINE = NCH // RADIX
LANES = 128
NA = 4
SPEC = 128
STEP = 32
BATCH = 8
SLOTS = 5
VMEM_KIB = 50 * 1024
HIST = TAPS - 1
ROWS = RADIX * NA
PITCH = ROWS + 8
GROUP = 64
PLANE = ("x", "z", "core")
PLANE_FIRST = (0, 1, 2, 3, 4)
Y_FIRST = (5, 6, 7)


def taps_table():
    k = jnp.arange(TAPS * NCH, dtype=jnp.float32)
    x = (k - 2.0 * NCH + 0.5) / NCH
    window = 0.54 - 0.46 * jnp.cos(2.0 * jnp.pi * (k + 0.5) / (TAPS * NCH))
    taps = (jnp.sinc(x) * window * 0.25).reshape(TAPS, RADIX, 1, LANES)
    return jnp.broadcast_to(taps, (TAPS, RADIX, NA, LANES)).reshape(TAPS, ROWS, LANES)


def turn_table():
    j = np.arange(RADIX)[:, None, None]
    q = np.arange(FINE)[None, :, None]
    l = np.arange(FINE)[None, None, :]
    angle = 2.0 * np.pi * ((l * (RADIX * q + j)) % NCH) / NCH
    cosine = np.cos(angle) / np.sqrt(NCH)
    sine = np.sin(angle) / np.sqrt(NCH)
    real = np.concatenate([cosine, sine], axis=2)
    imag = np.concatenate([-sine, cosine], axis=2)
    full = np.concatenate([real, imag], axis=1)
    high = full.astype(jnp.bfloat16)
    low = (full - high.astype(np.float64)).astype(jnp.bfloat16)
    blank = np.zeros_like(high)
    return np.stack([high, low, blank, blank], axis=1)


def gather_table():
    table = np.zeros((256, 256), np.float32)
    for p in range(2):
        for r in range(32):
            for a in range(NA):
                table[p * 128 + r * NA + a, r * 8 + p * NA + a] = 1.0
    return table.astype(jnp.bfloat16)


def butterfly(x):
    def add(u, v):
        return (u[0] + v[0], u[1] + v[1])

    def sub(u, v):
        return (u[0] - v[0], u[1] - v[1])

    def minus_i(u):
        return (u[1], -u[0])

    def four(a, b, c, d):
        s, t = add(a, c), sub(a, c)
        u, v = add(b, d), minus_i(sub(b, d))
        return add(s, u), add(t, v), sub(s, u), sub(t, v)

    half = np.float32(np.sqrt(0.5))
    even = four(x[0], x[2], x[4], x[6])
    odd = four(x[1], x[3], x[5], x[7])
    o1 = ((odd[1][0] + odd[1][1]) * half, (odd[1][1] - odd[1][0]) * half)
    o2 = minus_i(odd[2])
    o3 = ((odd[3][1] - odd[3][0]) * half, -(odd[3][0] + odd[3][1]) * half)
    odd = (odd[0], o1, o2, o3)
    return [add(even[i], odd[i]) for i in range(4)] + [sub(even[i], odd[i]) for i in range(4)]


def transform(mine, j, table, high, low, spread):
    def dot(left, right):
        return lax.dot_general(
            left, right, (((1,), (1,)), ((), ())), preferred_element_type=jnp.float32
        )

    rows = []
    for kind in range(2):
        pieces = []
        for p in range(2):
            for slot in range(2):
                half = mine if slot == 0 else 1 - mine
                start = pl.multiple_of(p * FINE + half * GROUP, GROUP)
                pieces.append(table[j, kind, pl.ds(start, GROUP), :])
        rows.append(jnp.concatenate(pieces, axis=0))
    tops = high[j]
    spectra = dot(rows[0], tops) + (dot(rows[1], tops) + dot(rows[0], low[j]))
    blocks = []
    for slot in range(2):
        for p in range(2):
            for a in range(NA):
                spread[
                    pl.ds(slot * GROUP * 8 + p * NA + a, GROUP, stride=8), :
                ] = spectra[
                    (p * 2 + slot) * GROUP : (p * 2 + slot + 1) * GROUP,
                    a * SPEC : (a + 1) * SPEC,
                ]
        block = spread[slot * GROUP * 8 : (slot + 1) * GROUP * 8, :]
        blocks.append(block.reshape(GROUP, 8, LANES).astype(jnp.bfloat16))
    return blocks


def channel_kernel(
    place, volts, tail, taps, turn, rest, late_high, late_low, raw, filt, high, low, table, spread, arrived
):
    def chunk_copy(c):
        at = pl.multiple_of(c * STEP * ROWS, STEP * ROWS)
        return pltpu.make_async_copy(
            volts.at[:, pl.ds(at, STEP * ROWS), :],
            raw.at[:, pl.ds(HIST * ROWS + at, STEP * ROWS), :],
            arrived.at[c],
        )

    table_copy = pltpu.make_async_copy(
        turn.at[pl.ds(0, len(PLANE_FIRST)), pl.ds(0, 2)], table, arrived.at[SPEC // STEP]
    )
    for c in range(SPEC // STEP):
        chunk_copy(c).start()
    table_copy.start()
    before = tail[...].astype(jnp.float32).astype(jnp.int32)
    raw[:, : HIST * ROWS, :] = jnp.where(place[1] > 0, before, 0)

    @pl.loop(0, SPEC // STEP)
    def _(c):
        chunk_copy(c).wait()
        for p in range(2):

            @pl.loop(0, STEP // BATCH)
            def _(i):
                into = pl.multiple_of(i * BATCH * ROWS, BATCH * ROWS)
                there = pl.multiple_of(i * BATCH * PITCH, BATCH * PITCH)
                base = pl.multiple_of(c * STEP * ROWS + into, BATCH * ROWS)
                for piece in range(ROWS // 8):
                    weights = [taps[t, piece * 8 : piece * 8 + 8, :] for t in range(TAPS)]
                    frames = [
                        raw[p, pl.ds(base + (s * ROWS + piece * 8), 8), :].astype(jnp.float32)
                        for s in range(BATCH + HIST)
                    ]
                    for s in range(BATCH):
                        total = weights[0] * frames[s]
                        for t in range(1, TAPS):
                            total = total + weights[t] * frames[s + t]
                        filt[p, pl.ds(there + (s * PITCH + piece * 8), 8), :] = total

        for a in range(NA):
            for part in range(STEP // 16):
                x = [
                    tuple(
                        filt[p, pl.ds(part * 16 * PITCH + m * NA + a, 16, stride=PITCH), :]
                        for p in range(2)
                    )
                    for m in range(RADIX)
                ]
                y = butterfly(x)
                row = pl.multiple_of(a * SPEC + c * STEP + part * 16, 16)
                for j in range(RADIX):
                    for p in range(2):
                        value = y[j][p]
                        top = value.astype(jnp.bfloat16)
                        left_over = (value - top.astype(jnp.float32)).astype(jnp.bfloat16)
                        at = (slice(p * LANES, (p + 1) * LANES),)
                        early = j < len(PLANE_FIRST)
                        here = j if early else j - len(PLANE_FIRST)
                        (high if early else late_high)[here, pl.ds(row, 16), *at] = top
                        (low if early else late_low)[here, pl.ds(row, 16), *at] = left_over

    table_copy.wait()
    for i in range(len(PLANE_FIRST)):
        blocks = transform(place[0], i, table, high, low, spread)
        for slot in range(2):
            rest[:, slot, i] = blocks[slot]


def late_kernel(place, turn, high, low, stay, leave, table, spread, arrived):
    table_copy = pltpu.make_async_copy(
        turn.at[pl.ds(len(PLANE_FIRST), len(Y_FIRST)), pl.ds(0, 2)], table, arrived
    )
    table_copy.start()
    table_copy.wait()
    for i in range(len(Y_FIRST)):
        stay[:, i], leave[:, i] = transform(place[0], i, table, high, low, spread)


def channelize(place, volts, tail, turn):
    few, many = len(Y_FIRST), len(PLANE_FIRST)
    vmem = pl.BlockSpec(memory_space=pltpu.VMEM)
    hbm = pl.BlockSpec(memory_space=pltpu.HBM)
    mixed = jax.ShapeDtypeStruct((few, NA * SPEC, 2 * LANES), jnp.bfloat16)
    return pl.pallas_call(
        channel_kernel,
        in_specs=[pl.BlockSpec(memory_space=pltpu.SMEM), hbm, vmem, vmem, hbm],
        out_specs=[vmem, vmem, vmem],
        scratch_shapes=[
            pltpu.VMEM((2, (HIST + SPEC) * ROWS, LANES), jnp.int32),
            pltpu.VMEM((2, STEP * PITCH, LANES), jnp.float32),
            pltpu.VMEM((many, NA * SPEC, 2 * LANES), jnp.bfloat16),
            pltpu.VMEM((many, NA * SPEC, 2 * LANES), jnp.bfloat16),
            pltpu.VMEM((many, 2, 2 * FINE, 2 * FINE), jnp.bfloat16),
            pltpu.VMEM((2 * GROUP * 8, LANES), jnp.float32),
            pltpu.SemaphoreType.DMA((SPEC // STEP + 1,)),
        ],
        out_shape=[jax.ShapeDtypeStruct((GROUP, 2, many, 8, LANES), jnp.bfloat16), mixed, mixed],
        compiler_params=pltpu.CompilerParams(vmem_limit_bytes=VMEM_KIB * 1024),
        cost_estimate=pl.CostEstimate(
            flops=2 * 10**9, bytes_accessed=8 * 1024 * 1024, transcendentals=0
        ),
        name="channelize",
    )(place, volts, tail, taps_table(), turn)


def channelize_late(place, turn, high, low):
    few = len(Y_FIRST)
    vmem = pl.BlockSpec(memory_space=pltpu.VMEM)
    hbm = pl.BlockSpec(memory_space=pltpu.HBM)
    block = jax.ShapeDtypeStruct((GROUP, few, 8, LANES), jnp.bfloat16)
    return pl.pallas_call(
        late_kernel,
        in_specs=[pl.BlockSpec(memory_space=pltpu.SMEM), hbm, vmem, vmem],
        out_specs=[vmem, vmem],
        scratch_shapes=[
            pltpu.VMEM((few, 2, 2 * FINE, 2 * FINE), jnp.bfloat16),
            pltpu.VMEM((2 * GROUP * 8, LANES), jnp.float32),
            pltpu.SemaphoreType.DMA(()),
        ],
        out_shape=[block, block],
        compiler_params=pltpu.CompilerParams(vmem_limit_bytes=24 * 1024 * 1024),
        cost_estimate=pl.CostEstimate(
            flops=6 * 10**8, bytes_accessed=3 * 1024 * 1024, transcendentals=0
        ),
        name="channelize_late",
    )(place, turn, high, low)


def correlate_kernel(scale, first, count, picks, place, *refs):
    operands, table, out = refs[: len(picks)], refs[len(picks)], refs[-3]
    held, sent = refs[-2:]
    mine, time = place[0], place[1]
    low_first = mine == 0

    def dot(left, right):
        return lax.dot_general(
            left, right, (((1,), (1,)), ((), ())), preferred_element_type=jnp.float32
        )

    def give(i, part):
        slot = i % SLOTS
        return pltpu.make_async_copy(
            held.at[slot, part], out.at[part, first + i], sent.at[slot, part]
        )

    for i in range(count):
        sets = []
        for kind in range(2):
            pair = [
                ref[:, at, i] if at is not None else ref[:, i]
                for ref, at in zip(operands[2 * kind : 2 * kind + 2], picks[2 * kind : 2 * kind + 2])
            ]
            pair = [block.reshape(GROUP * 8, LANES) for block in pair]
            parts = ([], [])
            for half in range(2):
                block = jnp.concatenate([b[half * 256 : half * 256 + 256] for b in pair], axis=1)
                ordered = jnp.dot(table[...], block, preferred_element_type=jnp.float32)
                ordered = ordered.astype(jnp.bfloat16)
                for p in range(2):
                    parts[p].append(ordered[p * 128 : p * 128 + 128])
            sets.append(jnp.concatenate([jnp.concatenate(part, axis=0) for part in parts], axis=1))
        columns = [jnp.where(low_first, sets[0], sets[1]), jnp.where(low_first, sets[1], sets[0])]
        rows = jnp.where(time == 0, columns[0], columns[1])
        turned = jnp.concatenate([rows[:, 256:], -rows[:, :256]], axis=1)

        slot = i % SLOTS
        for part, left in enumerate((rows, turned)):
            if i >= SLOTS:
                give(i - SLOTS, part).wait()
            for group in range(2):
                at = slice(group * 256, group * 256 + 256)
                held[slot, part, :, at] = dot(left, columns[group]) * scale
            give(i, part).start()
    for i in range(max(count - SLOTS, 0), count):
        for part in range(2):
            give(i, part).wait()


def correlate(place, scale, first, count, kinds, earlier):
    vmem = pl.BlockSpec(memory_space=pltpu.VMEM)
    hbm = pl.BlockSpec(memory_space=pltpu.HBM)
    picks = [at for _, at in kinds]
    operands = [place, *(block for block, _ in kinds), jnp.asarray(gather_table())]
    in_specs = [pl.BlockSpec(memory_space=pltpu.SMEM)] + [vmem] * (len(operands) - 1)
    aliases = {}
    if earlier is not None:
        in_specs.append(hbm)
        aliases = {len(operands): 0}
        operands.append(earlier)

    def kernel(*refs):
        correlate_kernel(scale, first, count, picks, *refs)

    return pl.pallas_call(
        kernel,
        in_specs=in_specs,
        out_specs=hbm,
        scratch_shapes=[
            pltpu.VMEM((SLOTS, 2, 256, 512), jnp.float32),
            pltpu.SemaphoreType.DMA((SLOTS, 2)),
        ],
        out_shape=jax.ShapeDtypeStruct((2, 8, 256, 512), jnp.float32),
        input_output_aliases=aliases,
        compiler_params=pltpu.CompilerParams(vmem_limit_bytes=24 * 1024 * 1024),
        cost_estimate=pl.CostEstimate(
            flops=count * 4 * 10**8, bytes_accessed=count * 3 * 512 * 1024, transcendentals=0
        ),
        name="correlate",
    )(*operands)


def exchange(near_part, far_part):
    flip = [(0, 1), (1, 0)]
    both = [(0, 3), (3, 0), (1, 2), (2, 1)]
    near = lax.ppermute(near_part, "y_lo", flip)
    cross = lax.ppermute(near_part, ("y_lo", "tm"), both)
    far = lax.ppermute(far_part, "tm", flip)
    return far, near, cross


def local(voltages):
    tiles = voltages.shape[2] // LANES
    volts = voltages.reshape(2, NA, tiles, LANES).transpose(0, 2, 1, 3).reshape(2, tiles * NA, LANES)
    tail = volts[:, (SPEC - HIST) * ROWS :].astype(jnp.bfloat16)
    tail = lax.ppermute(tail, "tm", [(0, 1), (1, 0)])
    place = jnp.stack([lax.axis_index("y_lo"), lax.axis_index("tm")]).astype(jnp.int32)
    scale = np.float32(1.0 / (SPEC * lax.axis_size("tm")))
    turn = jnp.asarray(turn_table())
    rest, high, low = channelize(place, volts, tail, turn)
    stay, leave = channelize_late(place, turn, high, low)
    over = lax.all_to_all(rest, PLANE, split_axis=0, concat_axis=0, tiled=True)
    early = jnp.stack([stay, *exchange(leave, stay)], axis=1)
    far, near, cross = exchange(over[:, 1], over[:, 0])
    early = lax.all_to_all(early, PLANE, split_axis=0, concat_axis=0, tiled=True)
    result = correlate(
        place, scale, 0, len(PLANE_FIRST), [(over, 0), (far, None), (near, None), (cross, None)], None
    )
    return correlate(
        place, scale, len(PLANE_FIRST), len(Y_FIRST), [(early, kind) for kind in range(4)], result
    )


def solution(mesh):
    names = ("y_lo", "x", "z", "core", "tm")
    fine = Mesh(mesh.devices.reshape(2, 4, 8, 2, 2), names)
    chan = names[:-1]
    return jax.shard_map(
        local,
        mesh=fine,
        in_specs=P(None, chan, "tm"),
        out_specs=P(None, chan, "tm", None),
        check_vma=False,
    )
```

```python
import jax
import jax.numpy as jnp
import numpy as np
from jax import lax
from jax.experimental import pallas as pl
from jax.experimental.pallas import tpu as pltpu
from jax.sharding import Mesh
from jax.sharding import PartitionSpec as P

NCH = 1024
TAPS = 4
RADIX = 8
FINE = NCH // RADIX
LANES = 128
NA = 4
SPEC = 128
STEP = 32
BODY = SPEC - STEP
BATCH = 8
SLOTS = 5
VMEM_KIB = 50 * 1024
MORE_KIB = 50 * 1024
HIST = TAPS - 1
ROWS = RADIX * NA
PITCH = ROWS + 8
GROUP = 64
PLANE = ("x", "z", "core")
PLANE_FIRST = (0, 1, 2, 3, 4)
Y_FIRST = (5, 6, 7)


def taps_table():
    k = jnp.arange(TAPS * NCH, dtype=jnp.float32)
    x = (k - 2.0 * NCH + 0.5) / NCH
    window = 0.54 - 0.46 * jnp.cos(2.0 * jnp.pi * (k + 0.5) / (TAPS * NCH))
    taps = (jnp.sinc(x) * window * 0.25).reshape(TAPS, RADIX, 1, LANES)
    return jnp.broadcast_to(taps, (TAPS, RADIX, NA, LANES)).reshape(TAPS, ROWS, LANES)


def turn_table():
    j = np.arange(RADIX)[:, None, None]
    q = np.arange(FINE)[None, :, None]
    l = np.arange(FINE)[None, None, :]
    angle = 2.0 * np.pi * ((l * (RADIX * q + j)) % NCH) / NCH
    cosine = np.cos(angle) / np.sqrt(NCH)
    sine = np.sin(angle) / np.sqrt(NCH)
    real = np.concatenate([cosine, sine], axis=2)
    imag = np.concatenate([-sine, cosine], axis=2)
    full = np.concatenate([real, imag], axis=1)
    high = full.astype(jnp.bfloat16)
    low = (full - high.astype(np.float64)).astype(jnp.bfloat16)
    blank = np.zeros_like(high)
    return np.stack([high, low, blank, blank], axis=1)


def gather_table():
    table = np.zeros((256, 256), np.float32)
    for p in range(2):
        for r in range(32):
            for a in range(NA):
                table[p * 128 + r * NA + a, r * 8 + p * NA + a] = 1.0
    return table.astype(jnp.bfloat16)


def butterfly(x):
    def add(u, v):
        return (u[0] + v[0], u[1] + v[1])

    def sub(u, v):
        return (u[0] - v[0], u[1] - v[1])

    def minus_i(u):
        return (u[1], -u[0])

    def four(a, b, c, d):
        s, t = add(a, c), sub(a, c)
        u, v = add(b, d), minus_i(sub(b, d))
        return add(s, u), add(t, v), sub(s, u), sub(t, v)

    half = np.float32(np.sqrt(0.5))
    even = four(x[0], x[2], x[4], x[6])
    odd = four(x[1], x[3], x[5], x[7])
    o1 = ((odd[1][0] + odd[1][1]) * half, (odd[1][1] - odd[1][0]) * half)
    o2 = minus_i(odd[2])
    o3 = ((odd[3][1] - odd[3][0]) * half, -(odd[3][0] + odd[3][1]) * half)
    odd = (odd[0], o1, o2, o3)
    return [add(even[i], odd[i]) for i in range(4)] + [sub(even[i], odd[i]) for i in range(4)]


def transform(mine, j, table, tops, lows, spread):
    def dot(left, right):
        return lax.dot_general(
            left, right, (((1,), (1,)), ((), ())), preferred_element_type=jnp.float32
        )

    rows = []
    for kind in range(2):
        pieces = []
        for p in range(2):
            for slot in range(2):
                half = mine if slot == 0 else 1 - mine
                start = pl.multiple_of(p * FINE + half * GROUP, GROUP)
                pieces.append(table[j, kind, pl.ds(start, GROUP), :])
        rows.append(jnp.concatenate(pieces, axis=0))
    spectra = dot(rows[0], tops) + (dot(rows[1], tops) + dot(rows[0], lows))
    blocks = []
    for slot in range(2):
        for p in range(2):
            for a in range(NA):
                spread[
                    pl.ds(slot * GROUP * 8 + p * NA + a, GROUP, stride=8), :
                ] = spectra[
                    (p * 2 + slot) * GROUP : (p * 2 + slot + 1) * GROUP,
                    a * SPEC : (a + 1) * SPEC,
                ]
        block = spread[slot * GROUP * 8 : (slot + 1) * GROUP * 8, :]
        blocks.append(block.reshape(GROUP, 8, LANES).astype(jnp.bfloat16))
    return blocks


def joined(head, body, j, k):
    parts = []
    for a in range(NA):
        parts.append(head[k, a * STEP : (a + 1) * STEP, :])
        parts.append(body[j, a * BODY : (a + 1) * BODY, :])
    return jnp.concatenate(parts, axis=0)


def mix(first, raw, taps, filt, store):
    for p in range(2):

        @pl.loop(0, STEP // BATCH)
        def _(i):
            base = pl.multiple_of(first + i * BATCH * ROWS, BATCH * ROWS)
            there = pl.multiple_of(i * BATCH * PITCH, BATCH * PITCH)
            for piece in range(ROWS // 8):
                weights = [taps[t, piece * 8 : piece * 8 + 8, :] for t in range(TAPS)]
                frames = [
                    raw[p, pl.ds(base + (s * ROWS + piece * 8), 8), :].astype(jnp.float32)
                    for s in range(BATCH + HIST)
                ]
                for s in range(BATCH):
                    total = weights[0] * frames[s]
                    for t in range(1, TAPS):
                        total = total + weights[t] * frames[s + t]
                    filt[p, pl.ds(there + (s * PITCH + piece * 8), 8), :] = total

    for a in range(NA):
        for part in range(STEP // 16):
            x = [
                tuple(
                    filt[p, pl.ds(part * 16 * PITCH + m * NA + a, 16, stride=PITCH), :]
                    for p in range(2)
                )
                for m in range(RADIX)
            ]
            y = butterfly(x)
            for j in range(RADIX):
                for p in range(2):
                    value = y[j][p]
                    top = value.astype(jnp.bfloat16)
                    left_over = (value - top.astype(jnp.float32)).astype(jnp.bfloat16)
                    store(j, a, part * 16, slice(p * LANES, (p + 1) * LANES), top, left_over)


def body_kernel(volts, taps, high, low, late_high, late_low, raw, filt, arrived):
    start = (STEP - HIST) * ROWS

    def chunk_copy(c):
        at = pl.multiple_of(c * STEP * ROWS, STEP * ROWS)
        return pltpu.make_async_copy(
            volts.at[:, pl.ds(STEP * ROWS + at, STEP * ROWS), :],
            raw.at[:, pl.ds(HIST * ROWS + at, STEP * ROWS), :],
            arrived.at[c],
        )

    before = pltpu.make_async_copy(
        volts.at[:, pl.ds(start, HIST * ROWS), :],
        raw.at[:, pl.ds(0, HIST * ROWS), :],
        arrived.at[BODY // STEP],
    )
    before.start()
    for c in range(BODY // STEP):
        chunk_copy(c).start()
    before.wait()

    @pl.loop(0, BODY // STEP)
    def _(c):
        chunk_copy(c).wait()

        def store(j, a, row, lanes, top, left_over):
            row = pl.multiple_of(a * BODY + c * STEP + row, 16)
            early = j < len(PLANE_FIRST)
            here = j if early else j - len(PLANE_FIRST)
            (high if early else late_high)[here, pl.ds(row, 16), lanes] = top
            (low if early else late_low)[here, pl.ds(row, 16), lanes] = left_over

        mix(c * STEP * ROWS, raw, taps, filt, store)


def channel_kernel(
    place, volts, tail, taps, turn, body_high, body_low, rest, late_high, late_low,
    raw, filt, high, low, table, spread, arrived,
):
    chunk = pltpu.make_async_copy(
        volts.at[:, pl.ds(0, STEP * ROWS), :],
        raw.at[:, pl.ds(HIST * ROWS, STEP * ROWS), :],
        arrived.at[0],
    )
    table_copy = pltpu.make_async_copy(
        turn.at[pl.ds(0, len(PLANE_FIRST)), pl.ds(0, 2)], table, arrived.at[1]
    )
    chunk.start()
    table_copy.start()
    before = tail[...].astype(jnp.float32).astype(jnp.int32)
    raw[:, : HIST * ROWS, :] = jnp.where(place[1] > 0, before, 0)
    chunk.wait()

    def store(j, a, row, lanes, top, left_over):
        early = j < len(PLANE_FIRST)
        here = j if early else j - len(PLANE_FIRST)
        row = a * STEP + row
        (high if early else late_high)[here, row : row + 16, lanes] = top
        (low if early else late_low)[here, row : row + 16, lanes] = left_over

    mix(0, raw, taps, filt, store)
    table_copy.wait()
    for i in range(len(PLANE_FIRST)):
        tops, lows = joined(high, body_high, i, i), joined(low, body_low, i, i)
        blocks = transform(place[0], i, table, tops, lows, spread)
        for slot in range(2):
            rest[:, slot, i] = blocks[slot]


def late_kernel(place, turn, body_high, body_low, high, low, stay, leave, table, spread, arrived):
    table_copy = pltpu.make_async_copy(
        turn.at[pl.ds(len(PLANE_FIRST), len(Y_FIRST)), pl.ds(0, 2)], table, arrived
    )
    table_copy.start()
    table_copy.wait()
    for i in range(len(Y_FIRST)):
        tops, lows = joined(high, body_high, i, i), joined(low, body_low, i, i)
        stay[:, i], leave[:, i] = transform(place[0], i, table, tops, lows, spread)


def channelize_body(volts, taps):
    vmem = pl.BlockSpec(memory_space=pltpu.VMEM)
    hbm = pl.BlockSpec(memory_space=pltpu.HBM)
    mixed = jax.ShapeDtypeStruct((len(PLANE_FIRST), NA * BODY, 2 * LANES), jnp.bfloat16)
    late = jax.ShapeDtypeStruct((len(Y_FIRST), NA * BODY, 2 * LANES), jnp.bfloat16)
    return pl.pallas_call(
        body_kernel,
        in_specs=[hbm, vmem],
        out_specs=[vmem] * 4,
        scratch_shapes=[
            pltpu.VMEM((2, (HIST + BODY) * ROWS, LANES), jnp.int32),
            pltpu.VMEM((2, STEP * PITCH, LANES), jnp.float32),
            pltpu.SemaphoreType.DMA((BODY // STEP + 1,)),
        ],
        out_shape=[mixed, mixed, late, late],
        compiler_params=pltpu.CompilerParams(vmem_limit_bytes=VMEM_KIB * 1024),
        cost_estimate=pl.CostEstimate(
            flops=10**9, bytes_accessed=8 * 1024 * 1024, transcendentals=0
        ),
        name="channelize_body",
    )(volts, taps)


def channelize(place, volts, tail, taps, turn, high, low):
    few, many = len(Y_FIRST), len(PLANE_FIRST)
    vmem = pl.BlockSpec(memory_space=pltpu.VMEM)
    hbm = pl.BlockSpec(memory_space=pltpu.HBM)
    mixed = jax.ShapeDtypeStruct((few, NA * STEP, 2 * LANES), jnp.bfloat16)
    return pl.pallas_call(
        channel_kernel,
        in_specs=[pl.BlockSpec(memory_space=pltpu.SMEM), hbm, vmem, vmem, hbm, vmem, vmem],
        out_specs=[vmem, vmem, vmem],
        scratch_shapes=[
            pltpu.VMEM((2, (HIST + STEP) * ROWS, LANES), jnp.int32),
            pltpu.VMEM((2, STEP * PITCH, LANES), jnp.float32),
            pltpu.VMEM((many, NA * STEP, 2 * LANES), jnp.bfloat16),
            pltpu.VMEM((many, NA * STEP, 2 * LANES), jnp.bfloat16),
            pltpu.VMEM((many, 2, 2 * FINE, 2 * FINE), jnp.bfloat16),
            pltpu.VMEM((2 * GROUP * 8, LANES), jnp.float32),
            pltpu.SemaphoreType.DMA((2,)),
        ],
        out_shape=[jax.ShapeDtypeStruct((GROUP, 2, many, 8, LANES), jnp.bfloat16), mixed, mixed],
        compiler_params=pltpu.CompilerParams(vmem_limit_bytes=MORE_KIB * 1024),
        cost_estimate=pl.CostEstimate(
            flops=10**9, bytes_accessed=6 * 1024 * 1024, transcendentals=0
        ),
        name="channelize",
    )(place, volts, tail, taps, turn, high, low)


def channelize_late(place, turn, body_high, body_low, high, low):
    few = len(Y_FIRST)
    vmem = pl.BlockSpec(memory_space=pltpu.VMEM)
    hbm = pl.BlockSpec(memory_space=pltpu.HBM)
    block = jax.ShapeDtypeStruct((GROUP, few, 8, LANES), jnp.bfloat16)
    return pl.pallas_call(
        late_kernel,
        in_specs=[pl.BlockSpec(memory_space=pltpu.SMEM), hbm, vmem, vmem, vmem, vmem],
        out_specs=[vmem, vmem],
        scratch_shapes=[
            pltpu.VMEM((few, 2, 2 * FINE, 2 * FINE), jnp.bfloat16),
            pltpu.VMEM((2 * GROUP * 8, LANES), jnp.float32),
            pltpu.SemaphoreType.DMA(()),
        ],
        out_shape=[block, block],
        compiler_params=pltpu.CompilerParams(vmem_limit_bytes=24 * 1024 * 1024),
        cost_estimate=pl.CostEstimate(
            flops=6 * 10**8, bytes_accessed=3 * 1024 * 1024, transcendentals=0
        ),
        name="channelize_late",
    )(place, turn, body_high, body_low, high, low)


def correlate_kernel(scale, first, count, picks, place, *refs):
    operands, table, out = refs[: len(picks)], refs[len(picks)], refs[-3]
    held, sent = refs[-2:]
    mine, time = place[0], place[1]
    low_first = mine == 0

    def dot(left, right):
        return lax.dot_general(
            left, right, (((1,), (1,)), ((), ())), preferred_element_type=jnp.float32
        )

    def give(i, part):
        slot = i % SLOTS
        return pltpu.make_async_copy(
            held.at[slot, part], out.at[part, first + i], sent.at[slot, part]
        )

    for i in range(count):
        sets = []
        for kind in range(2):
            pair = [
                ref[:, at, i] if at is not None else ref[:, i]
                for ref, at in zip(operands[2 * kind : 2 * kind + 2], picks[2 * kind : 2 * kind + 2])
            ]
            pair = [block.reshape(GROUP * 8, LANES) for block in pair]
            parts = ([], [])
            for half in range(2):
                block = jnp.concatenate([b[half * 256 : half * 256 + 256] for b in pair], axis=1)
                ordered = jnp.dot(table[...], block, preferred_element_type=jnp.float32)
                ordered = ordered.astype(jnp.bfloat16)
                for p in range(2):
                    parts[p].append(ordered[p * 128 : p * 128 + 128])
            sets.append(jnp.concatenate([jnp.concatenate(part, axis=0) for part in parts], axis=1))
        columns = [jnp.where(low_first, sets[0], sets[1]), jnp.where(low_first, sets[1], sets[0])]
        rows = jnp.where(time == 0, columns[0], columns[1])
        turned = jnp.concatenate([rows[:, 256:], -rows[:, :256]], axis=1)

        slot = i % SLOTS
        for part, left in enumerate((rows, turned)):
            if i >= SLOTS:
                give(i - SLOTS, part).wait()
            for group in range(2):
                at = slice(group * 256, group * 256 + 256)
                held[slot, part, :, at] = dot(left, columns[group]) * scale
            give(i, part).start()
    for i in range(max(count - SLOTS, 0), count):
        for part in range(2):
            give(i, part).wait()


def correlate(place, scale, first, count, kinds, earlier):
    vmem = pl.BlockSpec(memory_space=pltpu.VMEM)
    hbm = pl.BlockSpec(memory_space=pltpu.HBM)
    picks = [at for _, at in kinds]
    operands = [place, *(block for block, _ in kinds), jnp.asarray(gather_table())]
    in_specs = [pl.BlockSpec(memory_space=pltpu.SMEM)] + [vmem] * (len(operands) - 1)
    aliases = {}
    if earlier is not None:
        in_specs.append(hbm)
        aliases = {len(operands): 0}
        operands.append(earlier)

    def kernel(*refs):
        correlate_kernel(scale, first, count, picks, *refs)

    return pl.pallas_call(
        kernel,
        in_specs=in_specs,
        out_specs=hbm,
        scratch_shapes=[
            pltpu.VMEM((SLOTS, 2, 256, 512), jnp.float32),
            pltpu.SemaphoreType.DMA((SLOTS, 2)),
        ],
        out_shape=jax.ShapeDtypeStruct((2, 8, 256, 512), jnp.float32),
        input_output_aliases=aliases,
        compiler_params=pltpu.CompilerParams(vmem_limit_bytes=24 * 1024 * 1024),
        cost_estimate=pl.CostEstimate(
            flops=count * 4 * 10**8, bytes_accessed=count * 3 * 512 * 1024, transcendentals=0
        ),
        name="correlate",
    )(*operands)


def exchange(near_part, far_part):
    flip = [(0, 1), (1, 0)]
    both = [(0, 3), (3, 0), (1, 2), (2, 1)]
    near = lax.ppermute(near_part, "y_lo", flip)
    cross = lax.ppermute(near_part, ("y_lo", "tm"), both)
    far = lax.ppermute(far_part, "tm", flip)
    return far, near, cross


def local(voltages):
    tiles = voltages.shape[2] // LANES
    volts = voltages.reshape(2, NA, tiles, LANES).transpose(0, 2, 1, 3).reshape(2, tiles * NA, LANES)
    tail = volts[:, (SPEC - HIST) * ROWS :].astype(jnp.bfloat16)
    tail = lax.ppermute(tail, "tm", [(0, 1), (1, 0)])
    place = jnp.stack([lax.axis_index("y_lo"), lax.axis_index("tm")]).astype(jnp.int32)
    scale = np.float32(1.0 / (SPEC * lax.axis_size("tm")))
    turn = jnp.asarray(turn_table())
    taps = taps_table()
    body = channelize_body(volts, taps)
    rest, *head = channelize(place, volts, tail, taps, turn, *body[:2])
    stay, leave = channelize_late(place, turn, *body[2:], *head)
    over = lax.all_to_all(rest, PLANE, split_axis=0, concat_axis=0, tiled=True)
    early = jnp.stack([stay, *exchange(leave, stay)], axis=1)
    far, near, cross = exchange(over[:, 1], over[:, 0])
    early = lax.all_to_all(early, PLANE, split_axis=0, concat_axis=0, tiled=True)
    result = correlate(
        place, scale, 0, len(PLANE_FIRST), [(over, 0), (far, None), (near, None), (cross, None)], None
    )
    return correlate(
        place, scale, len(PLANE_FIRST), len(Y_FIRST), [(early, kind) for kind in range(4)], result
    )


def solution(mesh):
    names = ("y_lo", "x", "z", "core", "tm")
    fine = Mesh(mesh.devices.reshape(2, 4, 8, 2, 2), names)
    chan = names[:-1]
    return jax.shard_map(
        local,
        mesh=fine,
        in_specs=P(None, chan, "tm"),
        out_specs=P(None, chan, "tm", None),
        check_vma=False,
    )
```

```python
import jax
import jax.numpy as jnp
import numpy as np
from jax import lax
from jax.experimental import pallas as pl
from jax.experimental.pallas import tpu as pltpu
from jax.sharding import Mesh
from jax.sharding import PartitionSpec as P

NCH = 1024
TAPS = 4
RADIX = 8
FINE = NCH // RADIX
LANES = 128
NA = 4
SPEC = 128
STEP = 16
BODY = SPEC - STEP
BATCH = 8
SLOTS = 5
VMEM_KIB = 50 * 1024
MORE_KIB = 50 * 1024
HIST = TAPS - 1
ROWS = RADIX * NA
PITCH = ROWS + 8
GROUP = 64
PLANE = ("x", "z", "core")
PLANE_FIRST = (0, 1, 2, 3, 4)
Y_FIRST = (5, 6, 7)


def taps_table():
    k = jnp.arange(TAPS * NCH, dtype=jnp.float32)
    x = (k - 2.0 * NCH + 0.5) / NCH
    window = 0.54 - 0.46 * jnp.cos(2.0 * jnp.pi * (k + 0.5) / (TAPS * NCH))
    taps = (jnp.sinc(x) * window * 0.25).reshape(TAPS, RADIX, 1, LANES)
    return jnp.broadcast_to(taps, (TAPS, RADIX, NA, LANES)).reshape(TAPS, ROWS, LANES)


def turn_table():
    j = np.arange(RADIX)[:, None, None]
    q = np.arange(FINE)[None, :, None]
    l = np.arange(FINE)[None, None, :]
    angle = 2.0 * np.pi * ((l * (RADIX * q + j)) % NCH) / NCH
    cosine = np.cos(angle) / np.sqrt(NCH)
    sine = np.sin(angle) / np.sqrt(NCH)
    real = np.concatenate([cosine, sine], axis=2)
    imag = np.concatenate([-sine, cosine], axis=2)
    full = np.concatenate([real, imag], axis=1)
    high = full.astype(jnp.bfloat16)
    low = (full - high.astype(np.float64)).astype(jnp.bfloat16)
    blank = np.zeros_like(high)
    return np.stack([high, low, blank, blank], axis=1)


def gather_table():
    table = np.zeros((256, 256), np.float32)
    for p in range(2):
        for r in range(32):
            for a in range(NA):
                table[p * 128 + r * NA + a, r * 8 + p * NA + a] = 1.0
    return table.astype(jnp.bfloat16)


def butterfly(x):
    def add(u, v):
        return (u[0] + v[0], u[1] + v[1])

    def sub(u, v):
        return (u[0] - v[0], u[1] - v[1])

    def minus_i(u):
        return (u[1], -u[0])

    def four(a, b, c, d):
        s, t = add(a, c), sub(a, c)
        u, v = add(b, d), minus_i(sub(b, d))
        return add(s, u), add(t, v), sub(s, u), sub(t, v)

    half = np.float32(np.sqrt(0.5))
    even = four(x[0], x[2], x[4], x[6])
    odd = four(x[1], x[3], x[5], x[7])
    o1 = ((odd[1][0] + odd[1][1]) * half, (odd[1][1] - odd[1][0]) * half)
    o2 = minus_i(odd[2])
    o3 = ((odd[3][1] - odd[3][0]) * half, -(odd[3][0] + odd[3][1]) * half)
    odd = (odd[0], o1, o2, o3)
    return [add(even[i], odd[i]) for i in range(4)] + [sub(even[i], odd[i]) for i in range(4)]


def transform(mine, j, table, tops, lows, spread):
    def dot(left, right):
        return lax.dot_general(
            left, right, (((1,), (1,)), ((), ())), preferred_element_type=jnp.float32
        )

    rows = []
    for kind in range(2):
        pieces = []
        for p in range(2):
            for slot in range(2):
                half = mine if slot == 0 else 1 - mine
                start = pl.multiple_of(p * FINE + half * GROUP, GROUP)
                pieces.append(table[j, kind, pl.ds(start, GROUP), :])
        rows.append(jnp.concatenate(pieces, axis=0))
    spectra = dot(rows[0], tops) + (dot(rows[1], tops) + dot(rows[0], lows))
    blocks = []
    for slot in range(2):
        for p in range(2):
            for a in range(NA):
                spread[
                    pl.ds(slot * GROUP * 8 + p * NA + a, GROUP, stride=8), :
                ] = spectra[
                    (p * 2 + slot) * GROUP : (p * 2 + slot + 1) * GROUP,
                    a * SPEC : (a + 1) * SPEC,
                ]
        block = spread[slot * GROUP * 8 : (slot + 1) * GROUP * 8, :]
        blocks.append(block.reshape(GROUP, 8, LANES).astype(jnp.bfloat16))
    return blocks


def joined(head, body, j, k):
    parts = []
    for a in range(NA):
        parts.append(head[k, a * STEP : (a + 1) * STEP, :])
        parts.append(body[j, a * BODY : (a + 1) * BODY, :])
    return jnp.concatenate(parts, axis=0)


def mix(first, raw, taps, filt, store):
    for p in range(2):

        @pl.loop(0, STEP // BATCH)
        def _(i):
            base = pl.multiple_of(first + i * BATCH * ROWS, BATCH * ROWS)
            there = pl.multiple_of(i * BATCH * PITCH, BATCH * PITCH)
            for piece in range(ROWS // 8):
                weights = [taps[t, piece * 8 : piece * 8 + 8, :] for t in range(TAPS)]
                frames = [
                    raw[p, pl.ds(base + (s * ROWS + piece * 8), 8), :].astype(jnp.float32)
                    for s in range(BATCH + HIST)
                ]
                for s in range(BATCH):
                    total = weights[0] * frames[s]
                    for t in range(1, TAPS):
                        total = total + weights[t] * frames[s + t]
                    filt[p, pl.ds(there + (s * PITCH + piece * 8), 8), :] = total

    for a in range(NA):
        for part in range(STEP // 16):
            x = [
                tuple(
                    filt[p, pl.ds(part * 16 * PITCH + m * NA + a, 16, stride=PITCH), :]
                    for p in range(2)
                )
                for m in range(RADIX)
            ]
            y = butterfly(x)
            for j in range(RADIX):
                for p in range(2):
                    value = y[j][p]
                    top = value.astype(jnp.bfloat16)
                    left_over = (value - top.astype(jnp.float32)).astype(jnp.bfloat16)
                    store(j, a, part * 16, slice(p * LANES, (p + 1) * LANES), top, left_over)


def body_kernel(volts, taps, high, low, late_high, late_low, raw, filt, arrived):
    start = (STEP - HIST) * ROWS

    def chunk_copy(c):
        at = pl.multiple_of(c * STEP * ROWS, STEP * ROWS)
        return pltpu.make_async_copy(
            volts.at[:, pl.ds(STEP * ROWS + at, STEP * ROWS), :],
            raw.at[:, pl.ds(HIST * ROWS + at, STEP * ROWS), :],
            arrived.at[c],
        )

    before = pltpu.make_async_copy(
        volts.at[:, pl.ds(start, HIST * ROWS), :],
        raw.at[:, pl.ds(0, HIST * ROWS), :],
        arrived.at[BODY // STEP],
    )
    before.start()
    for c in range(BODY // STEP):
        chunk_copy(c).start()
    before.wait()

    @pl.loop(0, BODY // STEP)
    def _(c):
        chunk_copy(c).wait()

        def store(j, a, row, lanes, top, left_over):
            row = pl.multiple_of(a * BODY + c * STEP + row, 16)
            early = j < len(PLANE_FIRST)
            here = j if early else j - len(PLANE_FIRST)
            (high if early else late_high)[here, pl.ds(row, 16), lanes] = top
            (low if early else late_low)[here, pl.ds(row, 16), lanes] = left_over

        mix(c * STEP * ROWS, raw, taps, filt, store)


def channel_kernel(
    place, volts, tail, taps, turn, body_high, body_low, rest, late_high, late_low,
    raw, filt, high, low, table, spread, arrived,
):
    chunk = pltpu.make_async_copy(
        volts.at[:, pl.ds(0, STEP * ROWS), :],
        raw.at[:, pl.ds(HIST * ROWS, STEP * ROWS), :],
        arrived.at[0],
    )
    table_copy = pltpu.make_async_copy(
        turn.at[pl.ds(0, len(PLANE_FIRST)), pl.ds(0, 2)], table, arrived.at[1]
    )
    chunk.start()
    table_copy.start()
    before = tail[...].astype(jnp.float32).astype(jnp.int32)
    raw[:, : HIST * ROWS, :] = jnp.where(place[1] > 0, before, 0)
    chunk.wait()

    def store(j, a, row, lanes, top, left_over):
        early = j < len(PLANE_FIRST)
        here = j if early else j - len(PLANE_FIRST)
        row = a * STEP + row
        (high if early else late_high)[here, row : row + 16, lanes] = top
        (low if early else late_low)[here, row : row + 16, lanes] = left_over

    mix(0, raw, taps, filt, store)
    table_copy.wait()
    for i in range(len(PLANE_FIRST)):
        tops, lows = joined(high, body_high, i, i), joined(low, body_low, i, i)
        blocks = transform(place[0], i, table, tops, lows, spread)
        for slot in range(2):
            rest[:, slot, i] = blocks[slot]


def late_kernel(place, turn, body_high, body_low, high, low, stay, leave, table, spread, arrived):
    table_copy = pltpu.make_async_copy(
        turn.at[pl.ds(len(PLANE_FIRST), len(Y_FIRST)), pl.ds(0, 2)], table, arrived
    )
    table_copy.start()
    table_copy.wait()
    for i in range(len(Y_FIRST)):
        tops, lows = joined(high, body_high, i, i), joined(low, body_low, i, i)
        stay[:, i], leave[:, i] = transform(place[0], i, table, tops, lows, spread)


def channelize_body(volts, taps):
    vmem = pl.BlockSpec(memory_space=pltpu.VMEM)
    hbm = pl.BlockSpec(memory_space=pltpu.HBM)
    mixed = jax.ShapeDtypeStruct((len(PLANE_FIRST), NA * BODY, 2 * LANES), jnp.bfloat16)
    late = jax.ShapeDtypeStruct((len(Y_FIRST), NA * BODY, 2 * LANES), jnp.bfloat16)
    return pl.pallas_call(
        body_kernel,
        in_specs=[hbm, vmem],
        out_specs=[vmem] * 4,
        scratch_shapes=[
            pltpu.VMEM((2, (HIST + BODY) * ROWS, LANES), jnp.int32),
            pltpu.VMEM((2, STEP * PITCH, LANES), jnp.float32),
            pltpu.SemaphoreType.DMA((BODY // STEP + 1,)),
        ],
        out_shape=[mixed, mixed, late, late],
        compiler_params=pltpu.CompilerParams(vmem_limit_bytes=VMEM_KIB * 1024),
        cost_estimate=pl.CostEstimate(
            flops=10**9, bytes_accessed=8 * 1024 * 1024, transcendentals=0
        ),
        name="channelize_body",
    )(volts, taps)


def channelize(place, volts, tail, taps, turn, high, low):
    few, many = len(Y_FIRST), len(PLANE_FIRST)
    vmem = pl.BlockSpec(memory_space=pltpu.VMEM)
    hbm = pl.BlockSpec(memory_space=pltpu.HBM)
    mixed = jax.ShapeDtypeStruct((few, NA * STEP, 2 * LANES), jnp.bfloat16)
    return pl.pallas_call(
        channel_kernel,
        in_specs=[pl.BlockSpec(memory_space=pltpu.SMEM), hbm, vmem, vmem, hbm, vmem, vmem],
        out_specs=[vmem, vmem, vmem],
        scratch_shapes=[
            pltpu.VMEM((2, (HIST + STEP) * ROWS, LANES), jnp.int32),
            pltpu.VMEM((2, STEP * PITCH, LANES), jnp.float32),
            pltpu.VMEM((many, NA * STEP, 2 * LANES), jnp.bfloat16),
            pltpu.VMEM((many, NA * STEP, 2 * LANES), jnp.bfloat16),
            pltpu.VMEM((many, 2, 2 * FINE, 2 * FINE), jnp.bfloat16),
            pltpu.VMEM((2 * GROUP * 8, LANES), jnp.float32),
            pltpu.SemaphoreType.DMA((2,)),
        ],
        out_shape=[jax.ShapeDtypeStruct((GROUP, 2, many, 8, LANES), jnp.bfloat16), mixed, mixed],
        compiler_params=pltpu.CompilerParams(vmem_limit_bytes=MORE_KIB * 1024),
        cost_estimate=pl.CostEstimate(
            flops=10**9, bytes_accessed=6 * 1024 * 1024, transcendentals=0
        ),
        name="channelize",
    )(place, volts, tail, taps, turn, high, low)


def channelize_late(place, turn, body_high, body_low, high, low):
    few = len(Y_FIRST)
    vmem = pl.BlockSpec(memory_space=pltpu.VMEM)
    hbm = pl.BlockSpec(memory_space=pltpu.HBM)
    block = jax.ShapeDtypeStruct((GROUP, few, 8, LANES), jnp.bfloat16)
    return pl.pallas_call(
        late_kernel,
        in_specs=[pl.BlockSpec(memory_space=pltpu.SMEM), hbm, vmem, vmem, vmem, vmem],
        out_specs=[vmem, vmem],
        scratch_shapes=[
            pltpu.VMEM((few, 2, 2 * FINE, 2 * FINE), jnp.bfloat16),
            pltpu.VMEM((2 * GROUP * 8, LANES), jnp.float32),
            pltpu.SemaphoreType.DMA(()),
        ],
        out_shape=[block, block],
        compiler_params=pltpu.CompilerParams(vmem_limit_bytes=24 * 1024 * 1024),
        cost_estimate=pl.CostEstimate(
            flops=6 * 10**8, bytes_accessed=3 * 1024 * 1024, transcendentals=0
        ),
        name="channelize_late",
    )(place, turn, body_high, body_low, high, low)


def correlate_kernel(scale, first, count, picks, place, *refs):
    operands, table, out = refs[: len(picks)], refs[len(picks)], refs[-3]
    held, sent = refs[-2:]
    mine, time = place[0], place[1]
    low_first = mine == 0

    def dot(left, right):
        return lax.dot_general(
            left, right, (((1,), (1,)), ((), ())), preferred_element_type=jnp.float32
        )

    def give(i, part):
        slot = i % SLOTS
        return pltpu.make_async_copy(
            held.at[slot, part], out.at[part, first + i], sent.at[slot, part]
        )

    for i in range(count):
        sets = []
        for kind in range(2):
            pair = [
                ref[:, at, i] if at is not None else ref[:, i]
                for ref, at in zip(operands[2 * kind : 2 * kind + 2], picks[2 * kind : 2 * kind + 2])
            ]
            pair = [block.reshape(GROUP * 8, LANES) for block in pair]
            parts = ([], [])
            for half in range(2):
                block = jnp.concatenate([b[half * 256 : half * 256 + 256] for b in pair], axis=1)
                ordered = jnp.dot(table[...], block, preferred_element_type=jnp.float32)
                ordered = ordered.astype(jnp.bfloat16)
                for p in range(2):
                    parts[p].append(ordered[p * 128 : p * 128 + 128])
            sets.append(jnp.concatenate([jnp.concatenate(part, axis=0) for part in parts], axis=1))
        columns = [jnp.where(low_first, sets[0], sets[1]), jnp.where(low_first, sets[1], sets[0])]
        rows = jnp.where(time == 0, columns[0], columns[1])
        turned = jnp.concatenate([rows[:, 256:], -rows[:, :256]], axis=1)

        slot = i % SLOTS
        for part, left in enumerate((rows, turned)):
            if i >= SLOTS:
                give(i - SLOTS, part).wait()
            for group in range(2):
                at = slice(group * 256, group * 256 + 256)
                held[slot, part, :, at] = dot(left, columns[group]) * scale
            give(i, part).start()
    for i in range(max(count - SLOTS, 0), count):
        for part in range(2):
            give(i, part).wait()


def correlate(place, scale, first, count, kinds, earlier):
    vmem = pl.BlockSpec(memory_space=pltpu.VMEM)
    hbm = pl.BlockSpec(memory_space=pltpu.HBM)
    picks = [at for _, at in kinds]
    operands = [place, *(block for block, _ in kinds), jnp.asarray(gather_table())]
    in_specs = [pl.BlockSpec(memory_space=pltpu.SMEM)] + [vmem] * (len(operands) - 1)
    aliases = {}
    if earlier is not None:
        in_specs.append(hbm)
        aliases = {len(operands): 0}
        operands.append(earlier)

    def kernel(*refs):
        correlate_kernel(scale, first, count, picks, *refs)

    return pl.pallas_call(
        kernel,
        in_specs=in_specs,
        out_specs=hbm,
        scratch_shapes=[
            pltpu.VMEM((SLOTS, 2, 256, 512), jnp.float32),
            pltpu.SemaphoreType.DMA((SLOTS, 2)),
        ],
        out_shape=jax.ShapeDtypeStruct((2, 8, 256, 512), jnp.float32),
        input_output_aliases=aliases,
        compiler_params=pltpu.CompilerParams(vmem_limit_bytes=24 * 1024 * 1024),
        cost_estimate=pl.CostEstimate(
            flops=count * 4 * 10**8, bytes_accessed=count * 3 * 512 * 1024, transcendentals=0
        ),
        name="correlate",
    )(*operands)


def exchange(near_part, far_part):
    flip = [(0, 1), (1, 0)]
    both = [(0, 3), (3, 0), (1, 2), (2, 1)]
    near = lax.ppermute(near_part, "y_lo", flip)
    cross = lax.ppermute(near_part, ("y_lo", "tm"), both)
    far = lax.ppermute(far_part, "tm", flip)
    return far, near, cross


def local(voltages):
    tiles = voltages.shape[2] // LANES
    volts = voltages.reshape(2, NA, tiles, LANES).transpose(0, 2, 1, 3).reshape(2, tiles * NA, LANES)
    tail = volts[:, (SPEC - HIST) * ROWS :].astype(jnp.bfloat16)
    tail = lax.ppermute(tail, "tm", [(0, 1), (1, 0)])
    place = jnp.stack([lax.axis_index("y_lo"), lax.axis_index("tm")]).astype(jnp.int32)
    scale = np.float32(1.0 / (SPEC * lax.axis_size("tm")))
    turn = jnp.asarray(turn_table())
    taps = taps_table()
    body = channelize_body(volts, taps)
    rest, *head = channelize(place, volts, tail, taps, turn, *body[:2])
    stay, leave = channelize_late(place, turn, *body[2:], *head)
    over = lax.all_to_all(rest, PLANE, split_axis=0, concat_axis=0, tiled=True)
    early = jnp.stack([stay, *exchange(leave, stay)], axis=1)
    far, near, cross = exchange(over[:, 1], over[:, 0])
    early = lax.all_to_all(early, PLANE, split_axis=0, concat_axis=0, tiled=True)
    result = correlate(
        place, scale, 0, len(PLANE_FIRST), [(over, 0), (far, None), (near, None), (cross, None)], None
    )
    return correlate(
        place, scale, len(PLANE_FIRST), len(Y_FIRST), [(early, kind) for kind in range(4)], result
    )


def solution(mesh):
    names = ("y_lo", "x", "z", "core", "tm")
    fine = Mesh(mesh.devices.reshape(2, 4, 8, 2, 2), names)
    chan = names[:-1]
    return jax.shard_map(
        local,
        mesh=fine,
        in_specs=P(None, chan, "tm"),
        out_specs=P(None, chan, "tm", None),
        check_vma=False,
    )
```

```python
import jax
import jax.numpy as jnp
import numpy as np
from jax import lax
from jax.experimental import pallas as pl
from jax.experimental.pallas import tpu as pltpu
from jax.sharding import Mesh
from jax.sharding import PartitionSpec as P

NCH = 1024
TAPS = 4
RADIX = 8
FINE = NCH // RADIX
LANES = 128
NA = 4
SPEC = 128
STEP = 16
BODY = SPEC - STEP
BATCH = 16
SLOTS = 5
VMEM_KIB = 50 * 1024
MORE_KIB = 50 * 1024
HIST = TAPS - 1
ROWS = RADIX * NA
PITCH = ROWS + 8
GROUP = 64
PLANE = ("x", "z", "core")
PLANE_FIRST = (0, 1, 2, 3, 4)
Y_FIRST = (5, 6, 7)


def taps_table():
    k = jnp.arange(TAPS * NCH, dtype=jnp.float32)
    x = (k - 2.0 * NCH + 0.5) / NCH
    window = 0.54 - 0.46 * jnp.cos(2.0 * jnp.pi * (k + 0.5) / (TAPS * NCH))
    taps = (jnp.sinc(x) * window * 0.25).reshape(TAPS, RADIX, 1, LANES)
    return jnp.broadcast_to(taps, (TAPS, RADIX, NA, LANES)).reshape(TAPS, ROWS, LANES)


def turn_table():
    j = np.arange(RADIX)[:, None, None]
    q = np.arange(FINE)[None, :, None]
    l = np.arange(FINE)[None, None, :]
    angle = 2.0 * np.pi * ((l * (RADIX * q + j)) % NCH) / NCH
    cosine = np.cos(angle) / np.sqrt(NCH)
    sine = np.sin(angle) / np.sqrt(NCH)
    real = np.concatenate([cosine, sine], axis=2)
    imag = np.concatenate([-sine, cosine], axis=2)
    full = np.concatenate([real, imag], axis=1)
    high = full.astype(jnp.bfloat16)
    low = (full - high.astype(np.float64)).astype(jnp.bfloat16)
    blank = np.zeros_like(high)
    return np.stack([high, low, blank, blank], axis=1)


def gather_table():
    table = np.zeros((256, 256), np.float32)
    for p in range(2):
        for r in range(32):
            for a in range(NA):
                table[p * 128 + r * NA + a, r * 8 + p * NA + a] = 1.0
    return table.astype(jnp.bfloat16)


def butterfly(x):
    def add(u, v):
        return (u[0] + v[0], u[1] + v[1])

    def sub(u, v):
        return (u[0] - v[0], u[1] - v[1])

    def minus_i(u):
        return (u[1], -u[0])

    def four(a, b, c, d):
        s, t = add(a, c), sub(a, c)
        u, v = add(b, d), minus_i(sub(b, d))
        return add(s, u), add(t, v), sub(s, u), sub(t, v)

    half = np.float32(np.sqrt(0.5))
    even = four(x[0], x[2], x[4], x[6])
    odd = four(x[1], x[3], x[5], x[7])
    o1 = ((odd[1][0] + odd[1][1]) * half, (odd[1][1] - odd[1][0]) * half)
    o2 = minus_i(odd[2])
    o3 = ((odd[3][1] - odd[3][0]) * half, -(odd[3][0] + odd[3][1]) * half)
    odd = (odd[0], o1, o2, o3)
    return [add(even[i], odd[i]) for i in range(4)] + [sub(even[i], odd[i]) for i in range(4)]


def transform(mine, j, table, tops, lows, spread):
    def dot(left, right):
        return lax.dot_general(
            left, right, (((1,), (1,)), ((), ())), preferred_element_type=jnp.float32
        )

    rows = []
    for kind in range(2):
        pieces = []
        for p in range(2):
            for slot in range(2):
                half = mine if slot == 0 else 1 - mine
                start = pl.multiple_of(p * FINE + half * GROUP, GROUP)
                pieces.append(table[j, kind, pl.ds(start, GROUP), :])
        rows.append(jnp.concatenate(pieces, axis=0))
    spectra = dot(rows[0], tops) + (dot(rows[1], tops) + dot(rows[0], lows))
    blocks = []
    for slot in range(2):
        for p in range(2):
            for a in range(NA):
                spread[
                    pl.ds(slot * GROUP * 8 + p * NA + a, GROUP, stride=8), :
                ] = spectra[
                    (p * 2 + slot) * GROUP : (p * 2 + slot + 1) * GROUP,
                    a * SPEC : (a + 1) * SPEC,
                ]
        block = spread[slot * GROUP * 8 : (slot + 1) * GROUP * 8, :]
        blocks.append(block.reshape(GROUP, 8, LANES).astype(jnp.bfloat16))
    return blocks


def joined(head, body, j, k):
    parts = []
    for a in range(NA):
        parts.append(head[k, a * STEP : (a + 1) * STEP, :])
        parts.append(body[j, a * BODY : (a + 1) * BODY, :])
    return jnp.concatenate(parts, axis=0)


def mix(first, raw, taps, filt, store):
    for p in range(2):

        @pl.loop(0, STEP // BATCH)
        def _(i):
            base = pl.multiple_of(first + i * BATCH * ROWS, BATCH * ROWS)
            there = pl.multiple_of(i * BATCH * PITCH, BATCH * PITCH)
            for piece in range(ROWS // 8):
                weights = [taps[t, piece * 8 : piece * 8 + 8, :] for t in range(TAPS)]
                frames = [
                    raw[p, pl.ds(base + (s * ROWS + piece * 8), 8), :].astype(jnp.float32)
                    for s in range(BATCH + HIST)
                ]
                for s in range(BATCH):
                    total = weights[0] * frames[s]
                    for t in range(1, TAPS):
                        total = total + weights[t] * frames[s + t]
                    filt[p, pl.ds(there + (s * PITCH + piece * 8), 8), :] = total

    for a in range(NA):
        for part in range(STEP // 16):
            x = [
                tuple(
                    filt[p, pl.ds(part * 16 * PITCH + m * NA + a, 16, stride=PITCH), :]
                    for p in range(2)
                )
                for m in range(RADIX)
            ]
            y = butterfly(x)
            for j in range(RADIX):
                for p in range(2):
                    value = y[j][p]
                    top = value.astype(jnp.bfloat16)
                    left_over = (value - top.astype(jnp.float32)).astype(jnp.bfloat16)
                    store(j, a, part * 16, slice(p * LANES, (p + 1) * LANES), top, left_over)


def body_kernel(volts, taps, high, low, late_high, late_low, raw, filt, arrived):
    start = (STEP - HIST) * ROWS

    def chunk_copy(c):
        at = pl.multiple_of(c * STEP * ROWS, STEP * ROWS)
        return pltpu.make_async_copy(
            volts.at[:, pl.ds(STEP * ROWS + at, STEP * ROWS), :],
            raw.at[:, pl.ds(HIST * ROWS + at, STEP * ROWS), :],
            arrived.at[c],
        )

    before = pltpu.make_async_copy(
        volts.at[:, pl.ds(start, HIST * ROWS), :],
        raw.at[:, pl.ds(0, HIST * ROWS), :],
        arrived.at[BODY // STEP],
    )
    before.start()
    for c in range(BODY // STEP):
        chunk_copy(c).start()
    before.wait()

    @pl.loop(0, BODY // STEP)
    def _(c):
        chunk_copy(c).wait()

        def store(j, a, row, lanes, top, left_over):
            row = pl.multiple_of(a * BODY + c * STEP + row, 16)
            early = j < len(PLANE_FIRST)
            here = j if early else j - len(PLANE_FIRST)
            (high if early else late_high)[here, pl.ds(row, 16), lanes] = top
            (low if early else late_low)[here, pl.ds(row, 16), lanes] = left_over

        mix(c * STEP * ROWS, raw, taps, filt, store)


def channel_kernel(
    place, volts, tail, taps, turn, body_high, body_low, rest, late_high, late_low,
    raw, filt, high, low, table, spread, arrived,
):
    chunk = pltpu.make_async_copy(
        volts.at[:, pl.ds(0, STEP * ROWS), :],
        raw.at[:, pl.ds(HIST * ROWS, STEP * ROWS), :],
        arrived.at[0],
    )
    table_copy = pltpu.make_async_copy(
        turn.at[pl.ds(0, len(PLANE_FIRST)), pl.ds(0, 2)], table, arrived.at[1]
    )
    chunk.start()
    table_copy.start()
    before = tail[...].astype(jnp.float32).astype(jnp.int32)
    raw[:, : HIST * ROWS, :] = jnp.where(place[1] > 0, before, 0)
    chunk.wait()

    def store(j, a, row, lanes, top, left_over):
        early = j < len(PLANE_FIRST)
        here = j if early else j - len(PLANE_FIRST)
        row = a * STEP + row
        (high if early else late_high)[here, row : row + 16, lanes] = top
        (low if early else late_low)[here, row : row + 16, lanes] = left_over

    mix(0, raw, taps, filt, store)
    table_copy.wait()
    for i in range(len(PLANE_FIRST)):
        tops, lows = joined(high, body_high, i, i), joined(low, body_low, i, i)
        blocks = transform(place[0], i, table, tops, lows, spread)
        for slot in range(2):
            rest[:, slot, i] = blocks[slot]


def late_kernel(place, turn, body_high, body_low, high, low, stay, leave, table, spread, arrived):
    table_copy = pltpu.make_async_copy(
        turn.at[pl.ds(len(PLANE_FIRST), len(Y_FIRST)), pl.ds(0, 2)], table, arrived
    )
    table_copy.start()
    table_copy.wait()
    for i in range(len(Y_FIRST)):
        tops, lows = joined(high, body_high, i, i), joined(low, body_low, i, i)
        stay[:, i], leave[:, i] = transform(place[0], i, table, tops, lows, spread)


def channelize_body(volts, taps):
    vmem = pl.BlockSpec(memory_space=pltpu.VMEM)
    hbm = pl.BlockSpec(memory_space=pltpu.HBM)
    mixed = jax.ShapeDtypeStruct((len(PLANE_FIRST), NA * BODY, 2 * LANES), jnp.bfloat16)
    late = jax.ShapeDtypeStruct((len(Y_FIRST), NA * BODY, 2 * LANES), jnp.bfloat16)
    return pl.pallas_call(
        body_kernel,
        in_specs=[hbm, vmem],
        out_specs=[vmem] * 4,
        scratch_shapes=[
            pltpu.VMEM((2, (HIST + BODY) * ROWS, LANES), jnp.int32),
            pltpu.VMEM((2, STEP * PITCH, LANES), jnp.float32),
            pltpu.SemaphoreType.DMA((BODY // STEP + 1,)),
        ],
        out_shape=[mixed, mixed, late, late],
        compiler_params=pltpu.CompilerParams(vmem_limit_bytes=VMEM_KIB * 1024),
        cost_estimate=pl.CostEstimate(
            flops=10**9, bytes_accessed=8 * 1024 * 1024, transcendentals=0
        ),
        name="channelize_body",
    )(volts, taps)


def channelize(place, volts, tail, taps, turn, high, low):
    few, many = len(Y_FIRST), len(PLANE_FIRST)
    vmem = pl.BlockSpec(memory_space=pltpu.VMEM)
    hbm = pl.BlockSpec(memory_space=pltpu.HBM)
    mixed = jax.ShapeDtypeStruct((few, NA * STEP, 2 * LANES), jnp.bfloat16)
    return pl.pallas_call(
        channel_kernel,
        in_specs=[pl.BlockSpec(memory_space=pltpu.SMEM), hbm, vmem, vmem, hbm, vmem, vmem],
        out_specs=[vmem, vmem, vmem],
        scratch_shapes=[
            pltpu.VMEM((2, (HIST + STEP) * ROWS, LANES), jnp.int32),
            pltpu.VMEM((2, STEP * PITCH, LANES), jnp.float32),
            pltpu.VMEM((many, NA * STEP, 2 * LANES), jnp.bfloat16),
            pltpu.VMEM((many, NA * STEP, 2 * LANES), jnp.bfloat16),
            pltpu.VMEM((many, 2, 2 * FINE, 2 * FINE), jnp.bfloat16),
            pltpu.VMEM((2 * GROUP * 8, LANES), jnp.float32),
            pltpu.SemaphoreType.DMA((2,)),
        ],
        out_shape=[jax.ShapeDtypeStruct((GROUP, 2, many, 8, LANES), jnp.bfloat16), mixed, mixed],
        compiler_params=pltpu.CompilerParams(vmem_limit_bytes=MORE_KIB * 1024),
        cost_estimate=pl.CostEstimate(
            flops=10**9, bytes_accessed=6 * 1024 * 1024, transcendentals=0
        ),
        name="channelize",
    )(place, volts, tail, taps, turn, high, low)


def channelize_late(place, turn, body_high, body_low, high, low):
    few = len(Y_FIRST)
    vmem = pl.BlockSpec(memory_space=pltpu.VMEM)
    hbm = pl.BlockSpec(memory_space=pltpu.HBM)
    block = jax.ShapeDtypeStruct((GROUP, few, 8, LANES), jnp.bfloat16)
    return pl.pallas_call(
        late_kernel,
        in_specs=[pl.BlockSpec(memory_space=pltpu.SMEM), hbm, vmem, vmem, vmem, vmem],
        out_specs=[vmem, vmem],
        scratch_shapes=[
            pltpu.VMEM((few, 2, 2 * FINE, 2 * FINE), jnp.bfloat16),
            pltpu.VMEM((2 * GROUP * 8, LANES), jnp.float32),
            pltpu.SemaphoreType.DMA(()),
        ],
        out_shape=[block, block],
        compiler_params=pltpu.CompilerParams(vmem_limit_bytes=24 * 1024 * 1024),
        cost_estimate=pl.CostEstimate(
            flops=6 * 10**8, bytes_accessed=3 * 1024 * 1024, transcendentals=0
        ),
        name="channelize_late",
    )(place, turn, body_high, body_low, high, low)


def correlate_kernel(scale, first, count, picks, place, *refs):
    operands, table, out = refs[: len(picks)], refs[len(picks)], refs[-3]
    held, sent = refs[-2:]
    mine, time = place[0], place[1]
    low_first = mine == 0

    def dot(left, right):
        return lax.dot_general(
            left, right, (((1,), (1,)), ((), ())), preferred_element_type=jnp.float32
        )

    def give(i, part):
        slot = i % SLOTS
        return pltpu.make_async_copy(
            held.at[slot, part], out.at[part, first + i], sent.at[slot, part]
        )

    for i in range(count):
        sets = []
        for kind in range(2):
            pair = [
                ref[:, at, i] if at is not None else ref[:, i]
                for ref, at in zip(operands[2 * kind : 2 * kind + 2], picks[2 * kind : 2 * kind + 2])
            ]
            pair = [block.reshape(GROUP * 8, LANES) for block in pair]
            parts = ([], [])
            for half in range(2):
                block = jnp.concatenate([b[half * 256 : half * 256 + 256] for b in pair], axis=1)
                ordered = jnp.dot(table[...], block, preferred_element_type=jnp.float32)
                ordered = ordered.astype(jnp.bfloat16)
                for p in range(2):
                    parts[p].append(ordered[p * 128 : p * 128 + 128])
            sets.append(jnp.concatenate([jnp.concatenate(part, axis=0) for part in parts], axis=1))
        columns = [jnp.where(low_first, sets[0], sets[1]), jnp.where(low_first, sets[1], sets[0])]
        rows = jnp.where(time == 0, columns[0], columns[1])
        turned = jnp.concatenate([rows[:, 256:], -rows[:, :256]], axis=1)

        slot = i % SLOTS
        for part, left in enumerate((rows, turned)):
            if i >= SLOTS:
                give(i - SLOTS, part).wait()
            for group in range(2):
                at = slice(group * 256, group * 256 + 256)
                held[slot, part, :, at] = dot(left, columns[group]) * scale
            give(i, part).start()
    for i in range(max(count - SLOTS, 0), count):
        for part in range(2):
            give(i, part).wait()


def correlate(place, scale, first, count, kinds, earlier):
    vmem = pl.BlockSpec(memory_space=pltpu.VMEM)
    hbm = pl.BlockSpec(memory_space=pltpu.HBM)
    picks = [at for _, at in kinds]
    operands = [place, *(block for block, _ in kinds), jnp.asarray(gather_table())]
    in_specs = [pl.BlockSpec(memory_space=pltpu.SMEM)] + [vmem] * (len(operands) - 1)
    aliases = {}
    if earlier is not None:
        in_specs.append(hbm)
        aliases = {len(operands): 0}
        operands.append(earlier)

    def kernel(*refs):
        correlate_kernel(scale, first, count, picks, *refs)

    return pl.pallas_call(
        kernel,
        in_specs=in_specs,
        out_specs=hbm,
        scratch_shapes=[
            pltpu.VMEM((SLOTS, 2, 256, 512), jnp.float32),
            pltpu.SemaphoreType.DMA((SLOTS, 2)),
        ],
        out_shape=jax.ShapeDtypeStruct((2, 8, 256, 512), jnp.float32),
        input_output_aliases=aliases,
        compiler_params=pltpu.CompilerParams(vmem_limit_bytes=24 * 1024 * 1024),
        cost_estimate=pl.CostEstimate(
            flops=count * 4 * 10**8, bytes_accessed=count * 3 * 512 * 1024, transcendentals=0
        ),
        name="correlate",
    )(*operands)


def exchange(near_part, far_part):
    flip = [(0, 1), (1, 0)]
    both = [(0, 3), (3, 0), (1, 2), (2, 1)]
    near = lax.ppermute(near_part, "y_lo", flip)
    cross = lax.ppermute(near_part, ("y_lo", "tm"), both)
    far = lax.ppermute(far_part, "tm", flip)
    return far, near, cross


def local(voltages):
    tiles = voltages.shape[2] // LANES
    volts = voltages.reshape(2, NA, tiles, LANES).transpose(0, 2, 1, 3).reshape(2, tiles * NA, LANES)
    tail = volts[:, (SPEC - HIST) * ROWS :].astype(jnp.bfloat16)
    tail = lax.ppermute(tail, "tm", [(0, 1), (1, 0)])
    place = jnp.stack([lax.axis_index("y_lo"), lax.axis_index("tm")]).astype(jnp.int32)
    scale = np.float32(1.0 / (SPEC * lax.axis_size("tm")))
    turn = jnp.asarray(turn_table())
    taps = taps_table()
    body = channelize_body(volts, taps)
    rest, *head = channelize(place, volts, tail, taps, turn, *body[:2])
    stay, leave = channelize_late(place, turn, *body[2:], *head)
    over = lax.all_to_all(rest, PLANE, split_axis=0, concat_axis=0, tiled=True)
    early = jnp.stack([stay, *exchange(leave, stay)], axis=1)
    far, near, cross = exchange(over[:, 1], over[:, 0])
    early = lax.all_to_all(early, PLANE, split_axis=0, concat_axis=0, tiled=True)
    result = correlate(
        place, scale, 0, len(PLANE_FIRST), [(over, 0), (far, None), (near, None), (cross, None)], None
    )
    return correlate(
        place, scale, len(PLANE_FIRST), len(Y_FIRST), [(early, kind) for kind in range(4)], result
    )


def solution(mesh):
    names = ("y_lo", "x", "z", "core", "tm")
    fine = Mesh(mesh.devices.reshape(2, 4, 8, 2, 2), names)
    chan = names[:-1]
    return jax.shard_map(
        local,
        mesh=fine,
        in_specs=P(None, chan, "tm"),
        out_specs=P(None, chan, "tm", None),
        check_vma=False,
    )
```
